32 devices in a mesh: seq: 8 (over y, x, core), chan: 4 (over z).
Axes of the slice: x: 2, y: 2, z: 4, core: 2. Of those that a mesh axis runs over, the one named last changes fastest.
Arguments:
- signal: bfloat16 [1024, 2048], P('chan', 'seq'), may hold values from -6 to 6
- gating: bfloat16 [1024, 2048], P('chan', 'seq'), may hold values from -6 to 6
- filter_taps: float32 [1024, 2048], P('chan', 'seq'), may hold values from -6 to 6
- decay_rates: float32 [1024], P('chan'), may hold values from 0.00012207031 to 0.0078125
- out_weight: bfloat16 [1024, 2048], P(None, 'chan'), may hold values from -0.1875 to 0.1875
- out_grad: bfloat16 [2048, 2048], P('seq', 'chan'), may hold values from -1.5 to 1.5
Outputs:
- mixed_out: bfloat16 [2048, 2048], P('seq', 'chan')
- signal_grad: float32 [1024, 2048], P('chan', 'seq')
- gating_grad: float32 [1024, 2048], P('chan', 'seq')
- taps_grad: float32 [1024, 2048], P('chan', 'seq')
The draws below stay inside these ranges and needn't reach their ends.
All inputs are finite; a program needn't handle non-finite values.
Results may differ from the reference program's by a relative error of at most 0.013.
Values may be sent and summed in bfloat16 or wider, within the bound.
No kernel may reach another device: no remote copies, remote signals or barrier semaphores. Data moves between devices by JAX's collectives and lax.ppermute only.
A program may use at most 64 MiB of HBM per device.

```python
import math
import jax
import jax.numpy as jnp
from jax import lax

CH = 1024
DM = 2048
LEN = 2048


def steps_of(stream_key, extent, cuts, smallest, high):
    def one(axis_at, blocks):
        heights = jax.random.uniform(jax.random.fold_in(jax.random.fold_in(stream_key, 6), axis_at), (blocks,), jnp.float32, smallest / len(cuts), high / len(cuts))
        return jnp.repeat(jnp.exp(heights), extent[axis_at] // blocks).reshape((-1,) + (1,) * (len(extent) - axis_at - 1))

    factor_of = one(*cuts[0])
    for cut in cuts[1:]:
        factor_of = factor_of * one(*cut)
    return factor_of


def bell_draw(key, shape, spread, most, cuts=(), held_as=jnp.bfloat16):
    factor_of = steps_of(key, shape, cuts, -0.22, 0.18) if cuts else 1.0
    array = jax.random.normal(key, shape, jnp.float32) * spread * factor_of
    return jnp.minimum(jnp.maximum(array, -most), most).astype(held_as)


def setup_inputs(seed: int = 0) -> dict:
    arg_keys = jax.random.split(jax.random.key(seed), 7)
    return {
        "signal": bell_draw(arg_keys[0], (CH, LEN), 1.0, 6.0, ((0, 4), (1, 8))),
        "gating": bell_draw(arg_keys[1], (CH, LEN), 1.0, 6.0, ((0, 4), (1, 8))),
        "filter_taps": bell_draw(arg_keys[2], (CH, LEN), 1.0, 6.0, ((0, 4), (1, 8)), jnp.float32),
        "decay_rates": jnp.clip(jnp.exp(math.log(0.0078125) - 4.158883 * jax.random.uniform(arg_keys[3], (CH,), jnp.float32) ** steps_of(arg_keys[3], (CH,), ((0, 4),), -0.2, 0.2)), 0.00012207031, 0.0078125),
        "out_weight": bell_draw(arg_keys[4], (CH, DM), CH ** -0.5, 0.1875, ((1, 4),)),
        "out_grad": bell_draw(arg_keys[5], (LEN, DM), 0.25, 1.5, ((0, 8), (1, 4))),
    }


def reference(signal, gating, filter_taps, decay_rates, out_weight, out_grad):
    length = signal.shape[1]
    fft_length = 2 * length
    places = jnp.arange(length, dtype=jnp.int32).astype(jnp.float32)
    window = jnp.exp(-decay_rates[:, None] * places[None, :]) * jnp.sqrt(2.0 * decay_rates)[:, None]
    filters = filter_taps * window
    inputs = signal.astype(jnp.float32)

    def convolve(operands):
        first_row, second_row = operands
        product = jnp.fft.rfft(first_row, n=fft_length) * jnp.fft.rfft(second_row, n=fft_length)
        return jnp.fft.irfft(product, n=fft_length)[:length]

    def correlate(operands):
        first_row, second_row = operands
        product = jnp.fft.rfft(first_row, n=fft_length) * jnp.conj(jnp.fft.rfft(second_row, n=fft_length))
        return jnp.fft.irfft(product, n=fft_length)[:length]
    mixed = lax.map(convolve, (inputs, filters))
    gate_values = gating.astype(jnp.float32)
    gated_rows = (gate_values * mixed).astype(jnp.bfloat16)
    mixed_out = jnp.dot(gated_rows.T, out_weight, preferred_element_type=jnp.float32).astype(jnp.bfloat16)
    grad_mixed_out = jnp.dot(out_weight, out_grad.T, preferred_element_type=jnp.float32)
    gating_grad = grad_mixed_out * mixed
    grad_mixed = grad_mixed_out * gate_values
    signal_grad = lax.map(correlate, (grad_mixed, filters))
    taps_grad = lax.map(correlate, (grad_mixed, inputs)) * window
    return (mixed_out, signal_grad, gating_grad, taps_grad)
```

```python
import functools

import jax
import jax.numpy as jnp
import ml_dtypes
import numpy as np
from jax import lax
from jax.experimental import pallas as pl
from jax.experimental.pallas import tpu as pltpu
from jax.sharding import PartitionSpec as P

f32 = jnp.float32
bf16 = jnp.bfloat16
VMEM = pl.BlockSpec(memory_space=pltpu.VMEM)
ROWS = 16
LANES = 128


def call(kernel, out_shape, count, scratch=(), flops=0, moved=0):
    return pl.pallas_call(
        kernel,
        out_shape=out_shape,
        in_specs=[VMEM] * count,
        out_specs=jax.tree.map(lambda _: VMEM, out_shape),
        scratch_shapes=list(scratch),
        cost_estimate=pl.CostEstimate(flops=flops, bytes_accessed=moved, transcendentals=0),
        compiler_params=pltpu.CompilerParams(vmem_limit_bytes=48 * 1024 * 1024),
    )


def within_table(lanes):
    index = np.arange(lanes)
    angle = 2.0 * np.pi * (np.outer(index, index) % lanes) / lanes
    cos, sin = np.cos(angle), np.sin(angle)
    table = np.concatenate(
        [np.concatenate([cos, -sin], 1), np.concatenate([sin, cos], 1)], 0
    )
    return table.astype(ml_dtypes.bfloat16)


def twiddle_table(blocks, lanes):
    rows = np.arange(blocks + 1)[:, None]
    angle = 2.0 * np.pi * rows * np.arange(lanes)[None, :] / (2 * blocks * lanes)
    return np.stack([np.cos(angle), np.sin(angle)], 1).astype(np.float32)


def turned(real, imag, turn, size):
    angle = 2.0 * np.pi * turn / size
    cos, sin = float(np.cos(angle)), float(np.sin(angle))
    if turn == 0:
        return real, imag
    if abs(abs(cos) - abs(sin)) < 1e-9:
        root = abs(cos)
        cs, ss = (1 if cos > 0 else -1), (1 if sin > 0 else -1)
        first = real if cs > 0 else -real
        if cs == ss:
            return (root * cs) * (real - imag), (root * cs) * (real + imag)
        return (root * cs) * (real + imag), (root * cs) * (imag - real)
    return cos * real - sin * imag, sin * real + cos * imag


def real_forward(tiles, size):
    if size == 2:
        return [(tiles[0], None), (tiles[0], None)]
    even = real_forward(tiles[0::2], size // 2)
    odd = real_forward(tiles[1::2], size // 2)
    quarter = size // 4
    out = [None] * (size // 2 + 1)
    out[0] = (even[0][0] + odd[0][0], None)
    out[size // 2] = (even[0][0] - odd[0][0], None)
    for row in range(1, quarter):
        real, imag = turned(odd[row][0], odd[row][1], -row, size)
        out[row] = (even[row][0] + real, even[row][1] + imag)
        out[size // 2 - row] = (even[row][0] - real, imag - even[row][1])
    out[quarter] = (even[quarter][0], -odd[quarter][0])
    return out


def real_inverse(rows, size):
    if size == 2:
        return [rows[0][0] + rows[1][0]]
    quarter = size // 4
    even, odd = [], []
    for row in range(quarter + 1):
        real, imag = rows[row]
        if row == 0:
            last = rows[size // 2][0]
            even.append((real + last, None))
            odd.append((real - last, None))
        elif row == quarter:
            even.append((2.0 * real, None))
            odd.append((-2.0 * imag, None))
        else:
            far_real, far_imag = rows[size // 2 - row]
            even.append((real + far_real, imag - far_imag))
            odd.append(turned(real - far_real, imag + far_imag, row, size))
    firsts = real_inverse(even, size // 2)
    seconds = real_inverse(odd, size // 2)
    return [tile for pair in zip(firsts, seconds) for tile in pair]


def tile_slices(rows, lanes):
    for row in range(0, rows, ROWS):
        for lane in range(0, lanes, LANES):
            yield row, lane


def first_step(read, twiddle_ref, out_ref, base, blocks, rows, lanes):
    for row, lane in tile_slices(rows, lanes):
        tiles = [read(block, row, lane) for block in range(blocks)]
        for step, (real, imag) in enumerate(real_forward(tiles, 2 * blocks)):
            cos = twiddle_ref[step, 0:1, lane : lane + LANES]
            sin = twiddle_ref[step, 1:2, lane : lane + LANES]
            if step == 0:
                new_real, new_imag = real, jnp.zeros_like(real)
            elif imag is None:
                new_real, new_imag = real * cos, -real * sin
            else:
                new_real, new_imag = real * cos + imag * sin, imag * cos - real * sin
            at = base + step * rows + row
            out_ref[at : at + ROWS, lane : lane + LANES] = new_real.astype(bf16)
            out_ref[at : at + ROWS, lanes + lane : lanes + lane + LANES] = new_imag.astype(bf16)


def last_step(spec_ref, base, twiddle_ref, write, blocks, rows, lanes):
    scale = 1.0 / (2 * blocks * lanes)
    for row, lane in tile_slices(rows, lanes):
        steps = []
        for step in range(blocks + 1):
            at = base + step * rows + row
            imag = spec_ref[at : at + ROWS, lane : lane + LANES]
            real = spec_ref[at : at + ROWS, lanes + lane : lanes + lane + LANES]
            cos = twiddle_ref[step, 0:1, lane : lane + LANES] * scale
            sin = twiddle_ref[step, 1:2, lane : lane + LANES] * scale
            new_real = real * cos - imag * sin
            if step == 0 or step == blocks:
                steps.append((new_real, None))
            else:
                steps.append((new_real, imag * cos + real * sin))
        for block, tile in enumerate(real_inverse(steps, 2 * blocks)):
            write(block, row, lane, tile)


def tile_read(ref, base):
    def read(block, row, lane):
        at = base + row
        return ref[block, at : at + ROWS, lane : lane + LANES].astype(f32)

    return read


def tile_write(ref, base):
    def write(block, row, lane, tile):
        at = base + row
        ref[block, at : at + ROWS, lane : lane + LANES] = tile.astype(ref.dtype)

    return write


def product(first_real, first_imag, second_real, second_imag, out_ref, base, conjugate):
    rows, lanes = first_real.shape
    if conjugate:
        real = first_real * second_real + first_imag * second_imag
        imag = first_imag * second_real - first_real * second_imag
    else:
        real = first_real * second_real - first_imag * second_imag
        imag = first_real * second_imag + first_imag * second_real
    out_ref[base : base + rows, :lanes] = imag.astype(bf16)
    out_ref[base : base + rows, lanes:] = real.astype(bf16)


def convolve_kernel(pair_ref, table_ref, twiddle_ref, mixed_ref, spec_ref, left_ref, back_ref):
    blocks, rows, lanes = mixed_ref.shape
    height = (blocks + 1) * rows
    first_step(tile_read(pair_ref, 0), twiddle_ref, left_ref, 0, blocks, rows, lanes)
    first_step(tile_read(pair_ref, rows), twiddle_ref, left_ref, height, blocks, rows, lanes)
    spec_ref[...] = jnp.dot(left_ref[...], table_ref[...], preferred_element_type=f32)
    product(
        spec_ref[:height, :lanes],
        spec_ref[:height, lanes:],
        spec_ref[height:, :lanes],
        spec_ref[height:, lanes:],
        left_ref,
        0,
        False,
    )
    back_ref[...] = jnp.dot(left_ref[:height], table_ref[...], preferred_element_type=f32)
    last_step(back_ref, 0, twiddle_ref, tile_write(mixed_ref, 0), blocks, rows, lanes)


def correlate_kernel(grad_ref, spec_ref, table_ref, twiddle_ref, out_ref, left_ref, back_ref):
    blocks, rows, lanes = grad_ref.shape
    height = (blocks + 1) * rows
    first_step(tile_read(grad_ref, 0), twiddle_ref, left_ref, 0, blocks, rows, lanes)
    grad = jnp.dot(left_ref[:height], table_ref[...], preferred_element_type=f32)
    for base, other in ((0, height), (height, 0)):
        product(
            grad[:, :lanes],
            grad[:, lanes:],
            spec_ref[other : other + height, :lanes],
            spec_ref[other : other + height, lanes:],
            left_ref,
            base,
            True,
        )
    back_ref[...] = jnp.dot(left_ref[...], table_ref[...], preferred_element_type=f32)
    last_step(back_ref, 0, twiddle_ref, tile_write(out_ref, 0), blocks, rows, lanes)
    last_step(back_ref, height, twiddle_ref, tile_write(out_ref, rows), blocks, rows, lanes)


def window_kernel(decay_ref, taps_ref, signal_ref, pair_ref, window_ref):
    channels, length = taps_ref.shape
    shards, twice, _ = pair_ref.shape
    owned = twice // 2
    start = lax.axis_index("seq") * length
    places = (start + lax.broadcasted_iota(jnp.int32, (1, length), 1)).astype(f32)
    rates = jnp.broadcast_to(decay_ref[...], (length, channels)).T
    window = jnp.exp(-rates * places) * jnp.sqrt(2.0 * rates)
    window_ref[...] = window
    filters = (taps_ref[...] * window).astype(bf16)
    for shard in range(shards):
        rows = slice(shard * owned, (shard + 1) * owned)
        pair_ref[shard, :owned] = signal_ref[rows]
        pair_ref[shard, owned:] = filters[rows]


def spread_kernel(weight_ref, grad_ref, *out_refs):
    count = len(out_refs)
    rows = weight_ref.shape[0] // count
    me = lax.axis_index("chan")
    for step in list(range(1, count)) + [0]:
        place = lax.rem(me + step, count)
        block = weight_ref[pl.ds(pl.multiple_of(place * rows, rows), rows), :]
        out_refs[step][...] = lax.dot_general(
            block, grad_ref[...], (((1,), (1,)), ((), ())), preferred_element_type=f32
        ).astype(out_refs[step].dtype)


def project_kernel(weight_ref, *refs):
    gated_refs, out_ref = refs[:-1], refs[-1]
    count = len(gated_refs)
    rows = weight_ref.shape[0] // count
    me = lax.axis_index("chan")
    total = None
    for step in range(count):
        place = lax.rem(me + count - step, count)
        block = weight_ref[pl.ds(pl.multiple_of(place * rows, rows), rows), :]
        term = lax.dot_general(
            gated_refs[step][...], block, (((0,), (0,)), ((), ())), preferred_element_type=f32
        )
        total = term if total is None else total + term
    out_ref[...] = total.astype(out_ref.dtype)


def return_kernel(back_ref, window_ref, signal_ref, taps_ref):
    shards, twice, _ = back_ref.shape
    owned = twice // 2
    for shard in range(shards):
        rows = slice(shard * owned, (shard + 1) * owned)
        signal_ref[rows] = back_ref[shard, :owned].astype(f32)
        taps_ref[rows] = back_ref[shard, owned:].astype(f32) * window_ref[rows]


def padded(array, owned, held):
    if owned == held:
        return array
    blocks, rows, lanes = array.shape
    groups = array.reshape(blocks, rows // owned, owned, lanes)
    groups = jnp.pad(groups, ((0, 0), (0, 0), (0, held - owned), (0, 0)))
    return groups.reshape(blocks, -1, lanes)


def trimmed(array, owned, held):
    if owned == held:
        return array
    blocks, rows, lanes = array.shape
    return array.reshape(blocks, rows // held, held, lanes)[:, :, :owned].reshape(blocks, -1, lanes)


def exchange(array):
    return lax.all_to_all(array, "seq", split_axis=0, concat_axis=0, tiled=True)


def per_device(signal, gating, filter_taps, decay_rates, out_weight, out_grad):
    channels, length = signal.shape
    shards = lax.axis_size("seq")
    parts = lax.axis_size("chan")
    owned = channels // shards
    held = -(-owned // ROWS) * ROWS
    height = (shards + 1) * held
    table = jnp.asarray(within_table(length))
    twiddle = jnp.asarray(twiddle_table(shards, length))
    shape = jax.ShapeDtypeStruct
    pass_flops = 2 * height * (2 * length) ** 2

    def shift(array, step):
        return lax.ppermute(array, "chan", [(i, (i + step) % parts) for i in range(parts)])

    pairs, window = call(
        window_kernel,
        (shape((shards, 2 * held, length), bf16), shape((channels, length), f32)),
        3,
    )(decay_rates.reshape(1, channels), filter_taps, signal) if owned == held else window_plain(
        decay_rates, filter_taps, signal, shards
    )
    arrived = exchange(pairs)

    partial = call(
        spread_kernel,
        tuple(shape((channels, length), f32 if k == 0 else bf16) for k in range(parts)),
        2,
        flops=2 * out_weight.shape[0] * out_weight.shape[1] * length,
        moved=2 * out_weight.size,
    )(out_weight, out_grad)
    shares = [shift(partial[step], step) for step in range(1, parts)]

    mixed_owned, spectra = call(
        convolve_kernel,
        (shape((shards, held, length), bf16), shape((2 * height, 2 * length), f32)),
        3,
        (pltpu.VMEM((2 * height, 2 * length), bf16), pltpu.VMEM((height, 2 * length), f32)),
        flops=3 * pass_flops,
        moved=4 * 2 * height * 2 * length,
    )(padded(arrived, owned, held), table, twiddle)
    mixed = exchange(trimmed(mixed_owned, owned, held)).reshape(channels, length).astype(f32)

    gate_values = gating.astype(f32)
    grad_mixed_out = partial[0]
    for share in shares:
        grad_mixed_out = grad_mixed_out + share.astype(f32)
    grad_mixed = (grad_mixed_out * gate_values).astype(bf16)
    grad_whole = exchange(grad_mixed.reshape(shards, owned, length))

    gating_grad = grad_mixed_out * mixed
    gated = (gate_values * mixed).astype(bf16)
    gathered = [gated] + [shift(gated, step) for step in range(1, parts)]
    mixed_out = call(
        project_kernel,
        shape((length, out_weight.shape[1]), bf16),
        1 + parts,
        flops=2 * out_weight.shape[0] * out_weight.shape[1] * length,
        moved=2 * out_weight.size,
    )(out_weight, *gathered)

    grads_owned = call(
        correlate_kernel,
        shape((shards, 2 * held, length), bf16),
        4,
        (pltpu.VMEM((2 * height, 2 * length), bf16), pltpu.VMEM((2 * height, 2 * length), f32)),
        flops=3 * pass_flops,
        moved=4 * 2 * height * 2 * length,
    )(padded(grad_whole, owned, held), spectra, table, twiddle)
    returned = exchange(trimmed(grads_owned, owned, held))
    if owned == held:
        signal_grad, taps_grad = call(
            return_kernel,
            (shape((channels, length), f32), shape((channels, length), f32)),
            2,
        )(returned, window)
    else:
        both = returned.reshape(shards, 2, owned, length).astype(f32)
        signal_grad = both[:, 0].reshape(channels, length)
        taps_grad = both[:, 1].reshape(channels, length) * window
    return (mixed_out, signal_grad, gating_grad, taps_grad)


def window_plain(decay_rates, filter_taps, signal, shards):
    channels, length = signal.shape
    owned = channels // shards
    places = (lax.axis_index("seq") * length + jnp.arange(length, dtype=jnp.int32)).astype(f32)
    rates = decay_rates[:, None]
    window = jnp.exp(-rates * places[None, :]) * jnp.sqrt(2.0 * rates)
    filters = (filter_taps * window).astype(bf16)
    pairs = jnp.stack(
        [signal.reshape(shards, owned, length), filters.reshape(shards, owned, length)], 1
    )
    return pairs.reshape(shards, 2 * owned, length), window


def solution(mesh):
    in_specs = (
        P("chan", "seq"),
        P("chan", "seq"),
        P("chan", "seq"),
        P("chan"),
        P(None, "chan"),
        P("seq", "chan"),
    )
    out_specs = (P("seq", "chan"), P("chan", "seq"), P("chan", "seq"), P("chan", "seq"))
    return jax.shard_map(
        per_device, mesh=mesh, in_specs=in_specs, out_specs=out_specs, check_vma=False
    )
```

```python
import functools

import jax
import jax.numpy as jnp
import ml_dtypes
import numpy as np
from jax import lax
from jax.experimental import pallas as pl
from jax.experimental.pallas import tpu as pltpu
from jax.sharding import PartitionSpec as P

f32 = jnp.float32
bf16 = jnp.bfloat16
VMEM = pl.BlockSpec(memory_space=pltpu.VMEM)
ANY = pl.BlockSpec(memory_space=pl.ANY)
PEAK_FLOPS_A_MICRO = 1.15e9
ROWS = 16
LANES = 128


def call(kernel, out_shape, in_specs, scratch=(), micros=1, out_specs=None, moved=0, room=16):
    return pl.pallas_call(
        kernel,
        out_shape=out_shape,
        in_specs=in_specs,
        out_specs=jax.tree.map(lambda _: VMEM, out_shape) if out_specs is None else out_specs,
        scratch_shapes=list(scratch),
        cost_estimate=pl.CostEstimate(
            flops=int(micros * PEAK_FLOPS_A_MICRO), bytes_accessed=moved, transcendentals=0
        ),
        compiler_params=pltpu.CompilerParams(vmem_limit_bytes=room * 1024 * 1024),
    )


def within_table(lanes):
    index = np.arange(lanes)
    angle = 2.0 * np.pi * (np.outer(index, index) % lanes) / lanes
    cos, sin = np.cos(angle), np.sin(angle)
    table = np.concatenate(
        [np.concatenate([cos, -sin], 1), np.concatenate([sin, cos], 1)], 0
    )
    return table.astype(ml_dtypes.bfloat16)


def twiddle_table(blocks, lanes):
    rows = np.arange(blocks + 1)[:, None]
    angle = 2.0 * np.pi * rows * np.arange(lanes)[None, :] / (2 * blocks * lanes)
    return np.stack([np.cos(angle), np.sin(angle)], 1).astype(np.float32)


def turned(real, imag, turn, size):
    angle = 2.0 * np.pi * turn / size
    cos, sin = float(np.cos(angle)), float(np.sin(angle))
    if turn == 0:
        return real, imag
    if abs(abs(cos) - abs(sin)) < 1e-9:
        root = abs(cos)
        cs, ss = (1 if cos > 0 else -1), (1 if sin > 0 else -1)
        first = real if cs > 0 else -real
        if cs == ss:
            return (root * cs) * (real - imag), (root * cs) * (real + imag)
        return (root * cs) * (real + imag), (root * cs) * (imag - real)
    return cos * real - sin * imag, sin * real + cos * imag


def real_forward(tiles, size):
    if size == 2:
        return [(tiles[0], None), (tiles[0], None)]
    even = real_forward(tiles[0::2], size // 2)
    odd = real_forward(tiles[1::2], size // 2)
    quarter = size // 4
    out = [None] * (size // 2 + 1)
    out[0] = (even[0][0] + odd[0][0], None)
    out[size // 2] = (even[0][0] - odd[0][0], None)
    for row in range(1, quarter):
        real, imag = turned(odd[row][0], odd[row][1], -row, size)
        out[row] = (even[row][0] + real, even[row][1] + imag)
        out[size // 2 - row] = (even[row][0] - real, imag - even[row][1])
    out[quarter] = (even[quarter][0], -odd[quarter][0])
    return out


def real_inverse(rows, size):
    if size == 2:
        return [rows[0][0] + rows[1][0]]
    quarter = size // 4
    even, odd = [], []
    for row in range(quarter + 1):
        real, imag = rows[row]
        if row == 0:
            last = rows[size // 2][0]
            even.append((real + last, None))
            odd.append((real - last, None))
        elif row == quarter:
            even.append((2.0 * real, None))
            odd.append((-2.0 * imag, None))
        else:
            far_real, far_imag = rows[size // 2 - row]
            even.append((real + far_real, imag - far_imag))
            odd.append(turned(real - far_real, imag + far_imag, row, size))
    firsts = real_inverse(even, size // 2)
    seconds = real_inverse(odd, size // 2)
    return [tile for pair in zip(firsts, seconds) for tile in pair]


def tile_slices(rows, lanes):
    for row in range(0, rows, ROWS):
        for lane in range(0, lanes, LANES):
            yield row, lane


def first_step(read, twiddle_ref, out_ref, base, blocks, rows, lanes):
    for row, lane in tile_slices(rows, lanes):
        tiles = [read(block, row, lane) for block in range(blocks)]
        for step, (real, imag) in enumerate(real_forward(tiles, 2 * blocks)):
            cos = twiddle_ref[step, 0:1, lane : lane + LANES]
            sin = twiddle_ref[step, 1:2, lane : lane + LANES]
            if step == 0:
                new_real, new_imag = real, jnp.zeros_like(real)
            elif imag is None:
                new_real, new_imag = real * cos, -real * sin
            else:
                new_real, new_imag = real * cos + imag * sin, imag * cos - real * sin
            at = base + step * rows + row
            out_ref[at : at + ROWS, lane : lane + LANES] = new_real.astype(bf16)
            out_ref[at : at + ROWS, lanes + lane : lanes + lane + LANES] = new_imag.astype(bf16)


def last_step(spec_ref, base, twiddle_ref, write, blocks, rows, lanes):
    scale = 1.0 / (2 * blocks * lanes)
    for row, lane in tile_slices(rows, lanes):
        steps = []
        for step in range(blocks + 1):
            at = base + step * rows + row
            imag = spec_ref[at : at + ROWS, lane : lane + LANES]
            real = spec_ref[at : at + ROWS, lanes + lane : lanes + lane + LANES]
            cos = twiddle_ref[step, 0:1, lane : lane + LANES] * scale
            sin = twiddle_ref[step, 1:2, lane : lane + LANES] * scale
            new_real = real * cos - imag * sin
            if step == 0 or step == blocks:
                steps.append((new_real, None))
            else:
                steps.append((new_real, imag * cos + real * sin))
        for block, tile in enumerate(real_inverse(steps, 2 * blocks)):
            write(block, row, lane, tile)


def tile_read(ref, base):
    def read(block, row, lane):
        at = base + row
        return ref[block, at : at + ROWS, lane : lane + LANES].astype(f32)

    return read


def tile_write(ref, base):
    def write(block, row, lane, tile):
        at = base + row
        ref[block, at : at + ROWS, lane : lane + LANES] = tile.astype(ref.dtype)

    return write


def product(first_real, first_imag, second_real, second_imag, out_ref, base, conjugate):
    rows, lanes = first_real.shape
    if conjugate:
        real = first_real * second_real + first_imag * second_imag
        imag = first_imag * second_real - first_real * second_imag
    else:
        real = first_real * second_real - first_imag * second_imag
        imag = first_real * second_imag + first_imag * second_real
    out_ref[base : base + rows, :lanes] = imag.astype(bf16)
    out_ref[base : base + rows, lanes:] = real.astype(bf16)


def convolve_kernel(
    pair_ref,
    table_ref,
    twiddle_ref,
    mixed_ref,
    signal_real,
    signal_imag,
    filter_real,
    filter_imag,
    left_ref,
    back_ref,
):
    blocks, rows, lanes = mixed_ref.shape
    height = (blocks + 1) * rows
    first_step(tile_read(pair_ref, 0), twiddle_ref, left_ref, 0, blocks, rows, lanes)
    first_step(tile_read(pair_ref, rows), twiddle_ref, left_ref, height, blocks, rows, lanes)
    spectra = []
    for base, real_ref, imag_ref in (
        (0, signal_real, signal_imag),
        (height, filter_real, filter_imag),
    ):
        spectrum = jnp.dot(
            left_ref[base : base + height], table_ref[...], preferred_element_type=f32
        )
        real_ref[...] = spectrum[:, :lanes].astype(bf16)
        imag_ref[...] = spectrum[:, lanes:].astype(bf16)
        spectra.append(spectrum)
    product(
        spectra[0][:, :lanes],
        spectra[0][:, lanes:],
        spectra[1][:, :lanes],
        spectra[1][:, lanes:],
        left_ref,
        0,
        False,
    )
    back_ref[...] = jnp.dot(left_ref[:height], table_ref[...], preferred_element_type=f32)
    last_step(back_ref, 0, twiddle_ref, tile_write(mixed_ref, 0), blocks, rows, lanes)


def correlate_kernel(
    grad_ref,
    signal_real,
    signal_imag,
    filter_real,
    filter_imag,
    table_ref,
    twiddle_ref,
    out_ref,
    left_ref,
    back_ref,
):
    blocks, rows, lanes = grad_ref.shape
    height = (blocks + 1) * rows
    first_step(tile_read(grad_ref, 0), twiddle_ref, left_ref, 0, blocks, rows, lanes)
    grad = jnp.dot(left_ref[:height], table_ref[...], preferred_element_type=f32)
    for base, real_ref, imag_ref in (
        (0, filter_real, filter_imag),
        (height, signal_real, signal_imag),
    ):
        product(
            grad[:, :lanes],
            grad[:, lanes:],
            real_ref[...].astype(f32),
            imag_ref[...].astype(f32),
            left_ref,
            base,
            True,
        )
    back_ref[...] = jnp.dot(left_ref[...], table_ref[...], preferred_element_type=f32)
    last_step(back_ref, 0, twiddle_ref, tile_write(out_ref, 0), blocks, rows, lanes)
    last_step(back_ref, height, twiddle_ref, tile_write(out_ref, rows), blocks, rows, lanes)


def window_kernel(
    decay_in, taps_in, signal_in, pair_ref, window_ref, decay_ref, taps_ref, signal_ref, sems
):
    fetches = [
        pltpu.make_async_copy(source, target, sems.at[at])
        for at, (source, target) in enumerate(
            ((decay_in, decay_ref), (taps_in, taps_ref), (signal_in, signal_ref))
        )
    ]
    for fetch in fetches:
        fetch.start()
    channels, length = taps_ref.shape
    shards, twice, _ = pair_ref.shape
    owned = twice // 2
    start = lax.axis_index("seq") * length
    places = (start + lax.broadcasted_iota(jnp.int32, (1, length), 1)).astype(f32)
    fetches[0].wait()
    rates = jnp.broadcast_to(decay_ref[...], (length, channels)).T
    window = jnp.exp(-rates * places) * jnp.sqrt(2.0 * rates)
    window_ref[...] = window
    fetches[1].wait()
    fetches[2].wait()
    filters = (taps_ref[...] * window).astype(bf16)
    for shard in range(shards):
        rows = slice(shard * owned, (shard + 1) * owned)
        pair_ref[shard, :owned] = signal_ref[rows]
        pair_ref[shard, owned:] = filters[rows]


def spread_kernel(weight_ref, grad_ref, *out_refs):
    count = len(out_refs)
    rows = weight_ref.shape[0] // count
    me = lax.axis_index("chan")
    for step in list(range(1, count)) + [0]:
        place = lax.rem(me + step, count)
        block = weight_ref[pl.ds(pl.multiple_of(place * rows, rows), rows), :]
        out_refs[step][...] = lax.dot_general(
            block, grad_ref[...], (((1,), (1,)), ((), ())), preferred_element_type=f32
        ).astype(out_refs[step].dtype)


def gate_kernel(gating_ref, mixed_ref, *refs):
    gating_grad_ref, grad_mixed_ref, gated_ref = refs[-3:]
    total = refs[0][...].astype(f32)
    for share in refs[1:-3]:
        total = total + share[...].astype(f32)
    gates = gating_ref[...].astype(f32)
    mixed = mixed_ref[...].astype(f32)
    grad_mixed_ref[...] = (total * gates).astype(bf16)
    gated_ref[...] = (gates * mixed).astype(bf16)
    gating_grad_ref[...] = total * mixed


def project_kernel(weight_ref, *refs):
    gated_refs, out_ref = refs[:-1], refs[-1]
    count = len(gated_refs)
    rows = weight_ref.shape[0] // count
    me = lax.axis_index("chan")
    total = None
    for step in range(count):
        place = lax.rem(me + count - step, count)
        block = weight_ref[pl.ds(pl.multiple_of(place * rows, rows), rows), :]
        term = lax.dot_general(
            gated_refs[step][...], block, (((0,), (0,)), ((), ())), preferred_element_type=f32
        )
        total = term if total is None else total + term
    out_ref[...] = total.astype(out_ref.dtype)


def return_kernel(back_ref, window_ref, signal_ref, taps_ref):
    shards, twice, _ = back_ref.shape
    owned = twice // 2
    for shard in range(shards):
        rows = slice(shard * owned, (shard + 1) * owned)
        signal_ref[rows] = back_ref[shard, :owned].astype(f32)
        taps_ref[rows] = back_ref[shard, owned:].astype(f32) * window_ref[rows]


def padded(array, owned, held):
    if owned == held:
        return array
    blocks, rows, lanes = array.shape
    groups = array.reshape(blocks, rows // owned, owned, lanes)
    groups = jnp.pad(groups, ((0, 0), (0, 0), (0, held - owned), (0, 0)))
    return groups.reshape(blocks, -1, lanes)


def trimmed(array, owned, held):
    if owned == held:
        return array
    blocks, rows, lanes = array.shape
    return array.reshape(blocks, rows // held, held, lanes)[:, :, :owned].reshape(blocks, -1, lanes)


def exchange(array):
    return lax.all_to_all(array, "seq", split_axis=0, concat_axis=0, tiled=True)


def per_device(signal, gating, filter_taps, decay_rates, out_weight, out_grad):
    channels, length = signal.shape
    shards = lax.axis_size("seq")
    parts = lax.axis_size("chan")
    owned = channels // shards
    held = -(-owned // ROWS) * ROWS
    height = (shards + 1) * held
    table = jnp.asarray(within_table(length))
    twiddle = jnp.asarray(twiddle_table(shards, length))
    shape = jax.ShapeDtypeStruct

    def shift(array, step):
        return lax.ppermute(array, "chan", [(i, (i + step) % parts) for i in range(parts)])

    if owned == held:
        pairs, window = call(
            window_kernel,
            (shape((shards, 2 * owned, length), bf16), shape((channels, length), f32)),
            [ANY] * 3,
            (
                pltpu.VMEM((1, channels), f32),
                pltpu.VMEM((channels, length), f32),
                pltpu.VMEM((channels, length), bf16),
                pltpu.SemaphoreType.DMA((3,)),
            ),
            room=62,
        )(decay_rates.reshape(1, channels), filter_taps, signal)
    else:
        pairs, window = window_plain(decay_rates, filter_taps, signal, shards)
    arrived = exchange(pairs)

    partial = call(
        spread_kernel,
        tuple(shape((channels, length), bf16) for k in range(parts)),
        [VMEM] * 2,
        micros=1.0,
    )(out_weight, out_grad)
    shares = [shift(partial[step], step) for step in range(1, parts)]

    mixed_owned, *spectra = call(
        convolve_kernel,
        (shape((shards, held, length), bf16),) + 4 * (shape((height, length), bf16),),
        [VMEM] * 3,
        (
            pltpu.VMEM((2 * height, 2 * length), bf16),
            pltpu.VMEM((height, 2 * length), f32),
        ),
        micros=2.0,
    )(padded(arrived, owned, held), table, twiddle)
    mixed = exchange(trimmed(mixed_owned, owned, held)).reshape(channels, length)

    gating_grad, grad_mixed, gated = call(
        gate_kernel,
        (
            shape((channels, length), f32),
            shape((channels, length), bf16),
            shape((channels, length), bf16),
        ),
        [VMEM] * (3 + len(shares)),
    )(gating, mixed, partial[0], *shares)
    grad_whole = exchange(grad_mixed.reshape(shards, owned, length))
    gathered = [gated] + [shift(gated, step) for step in range(1, parts)]
    mixed_out = call(
        project_kernel,
        shape((length, out_weight.shape[1]), bf16),
        [VMEM] * (1 + parts),
        micros=12.0,
    )(out_weight, *gathered)

    grads_owned = call(
        correlate_kernel,
        shape((shards, 2 * held, length), bf16),
        [VMEM] * 7,
        (
            pltpu.VMEM((2 * height, 2 * length), bf16),
            pltpu.VMEM((2 * height, 2 * length), f32),
        ),
        micros=2.0,
    )(padded(grad_whole, owned, held), *spectra, table, twiddle)
    returned = exchange(trimmed(grads_owned, owned, held))
    if owned == held:
        signal_grad, taps_grad = call(
            return_kernel,
            (shape((channels, length), f32), shape((channels, length), f32)),
            [VMEM] * 2,
        )(returned, window)
    else:
        both = returned.reshape(shards, 2, owned, length).astype(f32)
        signal_grad = both[:, 0].reshape(channels, length)
        taps_grad = both[:, 1].reshape(channels, length) * window
    return (mixed_out, signal_grad, gating_grad, taps_grad)


def window_plain(decay_rates, filter_taps, signal, shards):
    channels, length = signal.shape
    owned = channels // shards
    places = (lax.axis_index("seq") * length + jnp.arange(length, dtype=jnp.int32)).astype(f32)
    rates = decay_rates[:, None]
    window = jnp.exp(-rates * places[None, :]) * jnp.sqrt(2.0 * rates)
    filters = (filter_taps * window).astype(bf16)
    pairs = jnp.stack(
        [signal.reshape(shards, owned, length), filters.reshape(shards, owned, length)], 1
    )
    return pairs.reshape(shards, 2 * owned, length), window


def solution(mesh):
    in_specs = (
        P("chan", "seq"),
        P("chan", "seq"),
        P("chan", "seq"),
        P("chan"),
        P(None, "chan"),
        P("seq", "chan"),
    )
    out_specs = (P("seq", "chan"), P("chan", "seq"), P("chan", "seq"), P("chan", "seq"))
    return jax.shard_map(
        per_device, mesh=mesh, in_specs=in_specs, out_specs=out_specs, check_vma=False
    )
```

```python
import functools

import jax
import jax.numpy as jnp
import ml_dtypes
import numpy as np
from jax import lax
from jax.experimental import pallas as pl
from jax.experimental.pallas import tpu as pltpu
from jax.sharding import PartitionSpec as P

f32 = jnp.float32
bf16 = jnp.bfloat16
VMEM = pl.BlockSpec(memory_space=pltpu.VMEM)
ANY = pl.BlockSpec(memory_space=pl.ANY)
PEAK_FLOPS_A_MICRO = 1.15e9
ROWS = 16
LANES = 128


def call(kernel, out_shape, in_specs, scratch=(), micros=1, room=16, after=()):
    count = len(in_specs)

    def body(*refs):
        kernel(*refs[:count], *refs[count + len(after) :])

    run = pl.pallas_call(
        body,
        out_shape=out_shape,
        in_specs=list(in_specs) + [ANY] * len(after),
        out_specs=jax.tree.map(lambda _: VMEM, out_shape),
        scratch_shapes=list(scratch),
        cost_estimate=pl.CostEstimate(
            flops=int(micros * PEAK_FLOPS_A_MICRO), bytes_accessed=0, transcendentals=0
        ),
        compiler_params=pltpu.CompilerParams(vmem_limit_bytes=room * 1024 * 1024),
    )
    return lambda *operands: run(*operands, *after)


def within_table(lanes):
    index = np.arange(lanes)
    angle = 2.0 * np.pi * (np.outer(index, index) % lanes) / lanes
    cos, sin = np.cos(angle), np.sin(angle)
    table = np.concatenate(
        [np.concatenate([cos, -sin], 1), np.concatenate([sin, cos], 1)], 0
    )
    return table.astype(ml_dtypes.bfloat16)


def twiddle_table(blocks, lanes):
    rows = np.arange(blocks + 1)[:, None]
    angle = 2.0 * np.pi * rows * np.arange(lanes)[None, :] / (2 * blocks * lanes)
    return np.stack([np.cos(angle), np.sin(angle)], 1).astype(np.float32)


def turned(real, imag, turn, size):
    angle = 2.0 * np.pi * turn / size
    cos, sin = float(np.cos(angle)), float(np.sin(angle))
    if turn == 0:
        return real, imag
    if abs(abs(cos) - abs(sin)) < 1e-9:
        root = abs(cos)
        cs, ss = (1 if cos > 0 else -1), (1 if sin > 0 else -1)
        first = real if cs > 0 else -real
        if cs == ss:
            return (root * cs) * (real - imag), (root * cs) * (real + imag)
        return (root * cs) * (real + imag), (root * cs) * (imag - real)
    return cos * real - sin * imag, sin * real + cos * imag


def real_forward(tiles, size):
    if size == 2:
        return [(tiles[0], None), (tiles[0], None)]
    even = real_forward(tiles[0::2], size // 2)
    odd = real_forward(tiles[1::2], size // 2)
    quarter = size // 4
    out = [None] * (size // 2 + 1)
    out[0] = (even[0][0] + odd[0][0], None)
    out[size // 2] = (even[0][0] - odd[0][0], None)
    for row in range(1, quarter):
        real, imag = turned(odd[row][0], odd[row][1], -row, size)
        out[row] = (even[row][0] + real, even[row][1] + imag)
        out[size // 2 - row] = (even[row][0] - real, imag - even[row][1])
    out[quarter] = (even[quarter][0], -odd[quarter][0])
    return out


def real_inverse(rows, size):
    if size == 2:
        return [rows[0][0] + rows[1][0]]
    quarter = size // 4
    even, odd = [], []
    for row in range(quarter + 1):
        real, imag = rows[row]
        if row == 0:
            last = rows[size // 2][0]
            even.append((real + last, None))
            odd.append((real - last, None))
        elif row == quarter:
            even.append((2.0 * real, None))
            odd.append((-2.0 * imag, None))
        else:
            far_real, far_imag = rows[size // 2 - row]
            even.append((real + far_real, imag - far_imag))
            odd.append(turned(real - far_real, imag + far_imag, row, size))
    firsts = real_inverse(even, size // 2)
    seconds = real_inverse(odd, size // 2)
    return [tile for pair in zip(firsts, seconds) for tile in pair]


def tile_slices(rows, lanes):
    for row in range(0, rows, ROWS):
        for lane in range(0, lanes, LANES):
            yield row, lane


def first_step(read, twiddle_ref, out_ref, base, blocks, rows, lanes):
    for row, lane in tile_slices(rows, lanes):
        tiles = [read(block, row, lane) for block in range(blocks)]
        for step, (real, imag) in enumerate(real_forward(tiles, 2 * blocks)):
            cos = twiddle_ref[step, 0:1, lane : lane + LANES]
            sin = twiddle_ref[step, 1:2, lane : lane + LANES]
            if step == 0:
                new_real, new_imag = real, jnp.zeros_like(real)
            elif imag is None:
                new_real, new_imag = real * cos, -real * sin
            else:
                new_real, new_imag = real * cos + imag * sin, imag * cos - real * sin
            at = base + step * rows + row
            out_ref[at : at + ROWS, lane : lane + LANES] = new_real.astype(bf16)
            out_ref[at : at + ROWS, lanes + lane : lanes + lane + LANES] = new_imag.astype(bf16)


def last_step(spec_ref, base, twiddle_ref, write, blocks, rows, lanes):
    scale = 1.0 / (2 * blocks * lanes)
    for row, lane in tile_slices(rows, lanes):
        steps = []
        for step in range(blocks + 1):
            at = base + step * rows + row
            imag = spec_ref[at : at + ROWS, lane : lane + LANES]
            real = spec_ref[at : at + ROWS, lanes + lane : lanes + lane + LANES]
            cos = twiddle_ref[step, 0:1, lane : lane + LANES] * scale
            sin = twiddle_ref[step, 1:2, lane : lane + LANES] * scale
            new_real = real * cos - imag * sin
            if step == 0 or step == blocks:
                steps.append((new_real, None))
            else:
                steps.append((new_real, imag * cos + real * sin))
        for block, tile in enumerate(real_inverse(steps, 2 * blocks)):
            write(block, row, lane, tile)


def tile_read(ref, base):
    def read(block, row, lane):
        at = base + row
        return ref[block, at : at + ROWS, lane : lane + LANES].astype(f32)

    return read


def tile_write(ref, base):
    def write(block, row, lane, tile):
        at = base + row
        ref[block, at : at + ROWS, lane : lane + LANES] = tile.astype(ref.dtype)

    return write


def product(first_real, first_imag, second_real, second_imag, out_ref, base, conjugate):
    rows, lanes = first_real.shape
    if conjugate:
        real = first_real * second_real + first_imag * second_imag
        imag = first_imag * second_real - first_real * second_imag
    else:
        real = first_real * second_real - first_imag * second_imag
        imag = first_real * second_imag + first_imag * second_real
    out_ref[base : base + rows, :lanes] = imag.astype(bf16)
    out_ref[base : base + rows, lanes:] = real.astype(bf16)


def convolve_kernel(
    pair_ref,
    table_ref,
    twiddle_ref,
    mixed_ref,
    signal_real,
    signal_imag,
    filter_real,
    filter_imag,
    left_ref,
    back_ref,
):
    blocks, rows, lanes = mixed_ref.shape
    height = (blocks + 1) * rows
    first_step(tile_read(pair_ref, 0), twiddle_ref, left_ref, 0, blocks, rows, lanes)
    first_step(tile_read(pair_ref, rows), twiddle_ref, left_ref, height, blocks, rows, lanes)
    spectra = []
    for base, real_ref, imag_ref in (
        (0, signal_real, signal_imag),
        (height, filter_real, filter_imag),
    ):
        spectrum = jnp.dot(
            left_ref[base : base + height], table_ref[...], preferred_element_type=f32
        )
        real_ref[...] = spectrum[:, :lanes].astype(bf16)
        imag_ref[...] = spectrum[:, lanes:].astype(bf16)
        spectra.append(spectrum)
    product(
        spectra[0][:, :lanes],
        spectra[0][:, lanes:],
        spectra[1][:, :lanes],
        spectra[1][:, lanes:],
        left_ref,
        0,
        False,
    )
    back_ref[...] = jnp.dot(left_ref[:height], table_ref[...], preferred_element_type=f32)
    last_step(back_ref, 0, twiddle_ref, tile_write(mixed_ref, 0), blocks, rows, lanes)


def correlate_kernel(
    grad_ref,
    signal_real,
    signal_imag,
    filter_real,
    filter_imag,
    table_ref,
    twiddle_ref,
    out_ref,
    left_ref,
    back_ref,
):
    blocks, rows, lanes = grad_ref.shape
    height = (blocks + 1) * rows
    first_step(tile_read(grad_ref, 0), twiddle_ref, left_ref, 0, blocks, rows, lanes)
    grad = jnp.dot(left_ref[:height], table_ref[...], preferred_element_type=f32)
    for base, real_ref, imag_ref in (
        (0, filter_real, filter_imag),
        (height, signal_real, signal_imag),
    ):
        product(
            grad[:, :lanes],
            grad[:, lanes:],
            real_ref[...].astype(f32),
            imag_ref[...].astype(f32),
            left_ref,
            base,
            True,
        )
    back_ref[...] = jnp.dot(left_ref[...], table_ref[...], preferred_element_type=f32)
    last_step(back_ref, 0, twiddle_ref, tile_write(out_ref, 0), blocks, rows, lanes)
    last_step(back_ref, height, twiddle_ref, tile_write(out_ref, rows), blocks, rows, lanes)


def window_kernel(
    decay_in, taps_in, signal_in, pair_ref, window_ref, decay_ref, taps_ref, signal_ref, sems
):
    fetches = [
        pltpu.make_async_copy(source, target, sems.at[at])
        for at, (source, target) in enumerate(
            ((decay_in, decay_ref), (taps_in, taps_ref), (signal_in, signal_ref))
        )
    ]
    for fetch in fetches:
        fetch.start()
    channels, length = taps_ref.shape
    shards, twice, _ = pair_ref.shape
    owned = twice // 2
    start = lax.axis_index("seq") * length
    places = (start + lax.broadcasted_iota(jnp.int32, (1, length), 1)).astype(f32)
    fetches[0].wait()
    rates = jnp.broadcast_to(decay_ref[...], (length, channels)).T
    window = jnp.exp(-rates * places) * jnp.sqrt(2.0 * rates)
    window_ref[...] = window
    fetches[1].wait()
    fetches[2].wait()
    filters = (taps_ref[...] * window).astype(bf16)
    for shard in range(shards):
        rows = slice(shard * owned, (shard + 1) * owned)
        pair_ref[shard, :owned] = signal_ref[rows]
        pair_ref[shard, owned:] = filters[rows]


def spread_kernel(weight_ref, grad_ref, *out_refs):
    count = len(out_refs)
    rows = weight_ref.shape[0] // count
    me = lax.axis_index("chan")
    for step in list(range(1, count)) + [0]:
        place = lax.rem(me + step, count)
        block = weight_ref[pl.ds(pl.multiple_of(place * rows, rows), rows), :]
        out_refs[step][...] = lax.dot_general(
            block, grad_ref[...], (((1,), (1,)), ((), ())), preferred_element_type=f32
        ).astype(out_refs[step].dtype)


def total_kernel(gating_ref, *refs):
    total_ref, grad_mixed_ref = refs[-2:]
    total = refs[0][...].astype(f32)
    for share in refs[1:-2]:
        total = total + share[...].astype(f32)
    total_ref[...] = total
    grad_mixed_ref[...] = (total * gating_ref[...].astype(f32)).astype(bf16)


def pack_kernel(both_ref, *out_refs):
    me = lax.axis_index("seq")
    core = lax.rem(me, 2)
    chip = lax.div(me, 2)
    for step, out_ref in enumerate(out_refs):
        block = 2 * lax.bitwise_xor(chip, step) + core
        for source in range(2):
            out_ref[source] = both_ref[source, block]


def gate_kernel(gating_ref, total_ref, *refs):
    gating_grad_ref, gated_ref = refs[-2:]
    pieces = refs[:-2]
    chip = lax.div(lax.axis_index("seq"), 2)
    count = gating_ref.shape[0] // len(pieces)
    for step, piece in enumerate(pieces):
        place = lax.bitwise_xor(chip, step) if len(pieces) > 1 else 0
        rows = pl.ds(pl.multiple_of(place * count, count), count)
        mixed = piece[...].reshape(count, -1).astype(f32)
        gated_ref[rows] = (gating_ref[rows].astype(f32) * mixed).astype(bf16)
        gating_grad_ref[rows] = total_ref[rows] * mixed


def project_kernel(weight_ref, *refs):
    gated_refs, out_ref = refs[:-1], refs[-1]
    count = len(gated_refs)
    rows = weight_ref.shape[0] // count
    me = lax.axis_index("chan")
    total = None
    for step in range(count):
        place = lax.rem(me + count - step, count)
        block = weight_ref[pl.ds(pl.multiple_of(place * rows, rows), rows), :]
        term = lax.dot_general(
            gated_refs[step][...], block, (((0,), (0,)), ((), ())), preferred_element_type=f32
        )
        total = term if total is None else total + term
    out_ref[...] = total.astype(out_ref.dtype)


def return_kernel(back_ref, window_ref, signal_ref, taps_ref):
    shards, twice, _ = back_ref.shape
    owned = twice // 2
    for shard in range(shards):
        rows = slice(shard * owned, (shard + 1) * owned)
        signal_ref[rows] = back_ref[shard, :owned].astype(f32)
        taps_ref[rows] = back_ref[shard, owned:].astype(f32) * window_ref[rows]


def padded(array, owned, held):
    if owned == held:
        return array
    blocks, rows, lanes = array.shape
    groups = array.reshape(blocks, rows // owned, owned, lanes)
    groups = jnp.pad(groups, ((0, 0), (0, 0), (0, held - owned), (0, 0)))
    return groups.reshape(blocks, -1, lanes)


def trimmed(array, owned, held):
    if owned == held:
        return array
    blocks, rows, lanes = array.shape
    return array.reshape(blocks, rows // held, held, lanes)[:, :, :owned].reshape(blocks, -1, lanes)


def exchange(array):
    return lax.all_to_all(array, "seq", split_axis=0, concat_axis=0, tiled=True)


def per_device(signal, gating, filter_taps, decay_rates, out_weight, out_grad):
    channels, length = signal.shape
    shards = lax.axis_size("seq")
    parts = lax.axis_size("chan")
    owned = channels // shards
    held = -(-owned // ROWS) * ROWS
    height = (shards + 1) * held
    table = jnp.asarray(within_table(length))
    twiddle = jnp.asarray(twiddle_table(shards, length))
    shape = jax.ShapeDtypeStruct

    def shift(array, step):
        return lax.ppermute(array, "chan", [(i, (i + step) % parts) for i in range(parts)])

    if owned == held:
        pairs, window = call(
            window_kernel,
            (shape((shards, 2 * owned, length), bf16), shape((channels, length), f32)),
            [ANY] * 3,
            (
                pltpu.VMEM((1, channels), f32),
                pltpu.VMEM((channels, length), f32),
                pltpu.VMEM((channels, length), bf16),
                pltpu.SemaphoreType.DMA((3,)),
            ),
            room=62,
        )(decay_rates.reshape(1, channels), filter_taps, signal)
    else:
        pairs, window = window_plain(decay_rates, filter_taps, signal, shards)
    arrived = exchange(pairs)

    partial = call(
        spread_kernel,
        tuple(shape((channels, length), bf16) for k in range(parts)),
        [VMEM] * 2,
        after=(pairs,),
    )(out_weight, out_grad)
    shares = [shift(partial[step], step) for step in range(1, parts)]

    mixed_owned, *spectra = call(
        convolve_kernel,
        (shape((shards, held, length), bf16),) + 4 * (shape((height, length), bf16),),
        [VMEM] * 3,
        (
            pltpu.VMEM((2 * height, 2 * length), bf16),
            pltpu.VMEM((height, 2 * length), f32),
        ),
        micros=2,
    )(padded(arrived, owned, held), table, twiddle)
    chips = shards // 2
    if chips in (2, 4) and owned == held:
        def hop(array, distance):
            return lax.ppermute(array, "seq", [(i, i ^ distance) for i in range(shards)])

        pairs = [[2 * chip, 2 * chip + 1] for chip in range(chips)]
        both = lax.all_gather(mixed_owned, "seq", axis_index_groups=pairs)
        pieces = call(
            pack_kernel,
            (shape((2, owned, length), bf16),) * chips,
            [VMEM],
        )(both)
        pieces = [pieces[0]] + [hop(pieces[step], 2 * step) for step in range(1, chips)]
    else:
        pieces = [exchange(trimmed(mixed_owned, owned, held)).reshape(channels, length)]

    total, grad_mixed = call(
        total_kernel,
        (shape((channels, length), f32), shape((channels, length), bf16)),
        [VMEM] * (2 + len(shares)),
        after=(pieces[0],),
    )(gating, partial[0], *shares)
    grad_whole = exchange(grad_mixed.reshape(shards, owned, length))

    gating_grad, gated = call(
        gate_kernel,
        (shape((channels, length), f32), shape((channels, length), bf16)),
        [VMEM] * (2 + len(pieces)),
    )(gating, total, *pieces)
    gathered = [gated] + [shift(gated, step) for step in range(1, parts)]
    mixed_out = call(
        project_kernel,
        shape((length, out_weight.shape[1]), bf16),
        [VMEM] * (1 + parts),
        micros=12.0,
    )(out_weight, *gathered)

    grads_owned = call(
        correlate_kernel,
        shape((shards, 2 * held, length), bf16),
        [VMEM] * 7,
        (
            pltpu.VMEM((2 * height, 2 * length), bf16),
            pltpu.VMEM((2 * height, 2 * length), f32),
        ),
        micros=2.0,
        after=(gated,),
    )(padded(grad_whole, owned, held), *spectra, table, twiddle)
    returned = exchange(trimmed(grads_owned, owned, held))
    if owned == held:
        signal_grad, taps_grad = call(
            return_kernel,
            (shape((channels, length), f32), shape((channels, length), f32)),
            [VMEM] * 2,
        )(returned, window)
    else:
        both = returned.reshape(shards, 2, owned, length).astype(f32)
        signal_grad = both[:, 0].reshape(channels, length)
        taps_grad = both[:, 1].reshape(channels, length) * window
    return (mixed_out, signal_grad, gating_grad, taps_grad)


def window_plain(decay_rates, filter_taps, signal, shards):
    channels, length = signal.shape
    owned = channels // shards
    places = (lax.axis_index("seq") * length + jnp.arange(length, dtype=jnp.int32)).astype(f32)
    rates = decay_rates[:, None]
    window = jnp.exp(-rates * places[None, :]) * jnp.sqrt(2.0 * rates)
    filters = (filter_taps * window).astype(bf16)
    pairs = jnp.stack(
        [signal.reshape(shards, owned, length), filters.reshape(shards, owned, length)], 1
    )
    return pairs.reshape(shards, 2 * owned, length), window


def solution(mesh):
    in_specs = (
        P("chan", "seq"),
        P("chan", "seq"),
        P("chan", "seq"),
        P("chan"),
        P(None, "chan"),
        P("seq", "chan"),
    )
    out_specs = (P("seq", "chan"), P("chan", "seq"), P("chan", "seq"), P("chan", "seq"))
    return jax.shard_map(
        per_device, mesh=mesh, in_specs=in_specs, out_specs=out_specs, check_vma=False
    )
```

```python
import functools

import jax
import jax.numpy as jnp
import ml_dtypes
import numpy as np
from jax import lax
from jax.experimental import pallas as pl
from jax.experimental.pallas import tpu as pltpu
from jax.sharding import PartitionSpec as P

f32 = jnp.float32
bf16 = jnp.bfloat16
VMEM = pl.BlockSpec(memory_space=pltpu.VMEM)
ANY = pl.BlockSpec(memory_space=pl.ANY)
PEAK_FLOPS_A_MICRO = 1.15e9
ROWS = 16
LANES = 128


def call(kernel, out_shape, in_specs, scratch=(), micros=1, room=16, after=()):
    count = len(in_specs)

    def body(*refs):
        kernel(*refs[:count], *refs[count + len(after) :])

    run = pl.pallas_call(
        body,
        out_shape=out_shape,
        in_specs=list(in_specs) + [ANY] * len(after),
        out_specs=jax.tree.map(lambda _: VMEM, out_shape),
        scratch_shapes=list(scratch),
        cost_estimate=pl.CostEstimate(
            flops=int(micros * PEAK_FLOPS_A_MICRO), bytes_accessed=0, transcendentals=0
        ),
        compiler_params=pltpu.CompilerParams(vmem_limit_bytes=room * 1024 * 1024),
    )
    return lambda *operands: run(*operands, *after)


def within_table(lanes):
    index = np.arange(lanes)
    angle = 2.0 * np.pi * (np.outer(index, index) % lanes) / lanes
    cos, sin = np.cos(angle), np.sin(angle)
    table = np.concatenate(
        [np.concatenate([cos, -sin], 1), np.concatenate([sin, cos], 1)], 0
    )
    return table.astype(ml_dtypes.bfloat16)


def twiddle_table(blocks, lanes):
    rows = np.arange(blocks + 1)[:, None]
    angle = 2.0 * np.pi * rows * np.arange(lanes)[None, :] / (2 * blocks * lanes)
    return np.stack([np.cos(angle), np.sin(angle)], 1).astype(np.float32)


def turned(real, imag, turn, size):
    angle = 2.0 * np.pi * turn / size
    cos, sin = float(np.cos(angle)), float(np.sin(angle))
    if turn == 0:
        return real, imag
    if abs(abs(cos) - abs(sin)) < 1e-9:
        root = abs(cos)
        cs, ss = (1 if cos > 0 else -1), (1 if sin > 0 else -1)
        first = real if cs > 0 else -real
        if cs == ss:
            return (root * cs) * (real - imag), (root * cs) * (real + imag)
        return (root * cs) * (real + imag), (root * cs) * (imag - real)
    return cos * real - sin * imag, sin * real + cos * imag


def real_forward(tiles, size):
    if size == 2:
        return [(tiles[0], None), (tiles[0], None)]
    even = real_forward(tiles[0::2], size // 2)
    odd = real_forward(tiles[1::2], size // 2)
    quarter = size // 4
    out = [None] * (size // 2 + 1)
    out[0] = (even[0][0] + odd[0][0], None)
    out[size // 2] = (even[0][0] - odd[0][0], None)
    for row in range(1, quarter):
        real, imag = turned(odd[row][0], odd[row][1], -row, size)
        out[row] = (even[row][0] + real, even[row][1] + imag)
        out[size // 2 - row] = (even[row][0] - real, imag - even[row][1])
    out[quarter] = (even[quarter][0], -odd[quarter][0])
    return out


def real_inverse(rows, size):
    if size == 2:
        return [rows[0][0] + rows[1][0]]
    quarter = size // 4
    even, odd = [], []
    for row in range(quarter + 1):
        real, imag = rows[row]
        if row == 0:
            last = rows[size // 2][0]
            even.append((real + last, None))
            odd.append((real - last, None))
        elif row == quarter:
            even.append((2.0 * real, None))
            odd.append((-2.0 * imag, None))
        else:
            far_real, far_imag = rows[size // 2 - row]
            even.append((real + far_real, imag - far_imag))
            odd.append(turned(real - far_real, imag + far_imag, row, size))
    firsts = real_inverse(even, size // 2)
    seconds = real_inverse(odd, size // 2)
    return [tile for pair in zip(firsts, seconds) for tile in pair]


def tile_slices(rows, lanes):
    for row in range(0, rows, ROWS):
        for lane in range(0, lanes, LANES):
            yield row, lane


def first_step(read, twiddle_ref, out_ref, base, blocks, rows, lanes):
    for row, lane in tile_slices(rows, lanes):
        tiles = [read(block, row, lane) for block in range(blocks)]
        for step, (real, imag) in enumerate(real_forward(tiles, 2 * blocks)):
            cos = twiddle_ref[step, 0:1, lane : lane + LANES]
            sin = twiddle_ref[step, 1:2, lane : lane + LANES]
            if step == 0:
                new_real, new_imag = real, jnp.zeros_like(real)
            elif imag is None:
                new_real, new_imag = real * cos, -real * sin
            else:
                new_real, new_imag = real * cos + imag * sin, imag * cos - real * sin
            at = base + step * rows + row
            out_ref[at : at + ROWS, lane : lane + LANES] = new_real.astype(bf16)
            out_ref[at : at + ROWS, lanes + lane : lanes + lane + LANES] = new_imag.astype(bf16)


def last_step(spec_ref, base, twiddle_ref, write, blocks, rows, lanes):
    scale = 1.0 / (2 * blocks * lanes)
    for row, lane in tile_slices(rows, lanes):
        steps = []
        for step in range(blocks + 1):
            at = base + step * rows + row
            imag = spec_ref[at : at + ROWS, lane : lane + LANES]
            real = spec_ref[at : at + ROWS, lanes + lane : lanes + lane + LANES]
            cos = twiddle_ref[step, 0:1, lane : lane + LANES] * scale
            sin = twiddle_ref[step, 1:2, lane : lane + LANES] * scale
            new_real = real * cos - imag * sin
            if step == 0 or step == blocks:
                steps.append((new_real, None))
            else:
                steps.append((new_real, imag * cos + real * sin))
        for block, tile in enumerate(real_inverse(steps, 2 * blocks)):
            write(block, row, lane, tile)


def tile_read(ref, base):
    def read(block, row, lane):
        at = base + row
        return ref[block, at : at + ROWS, lane : lane + LANES].astype(f32)

    return read


def tile_write(ref, base):
    def write(block, row, lane, tile):
        at = base + row
        ref[block, at : at + ROWS, lane : lane + LANES] = tile.astype(ref.dtype)

    return write


def product(first_real, first_imag, second_real, second_imag, out_ref, base, conjugate):
    rows, lanes = first_real.shape
    if conjugate:
        real = first_real * second_real + first_imag * second_imag
        imag = first_imag * second_real - first_real * second_imag
    else:
        real = first_real * second_real - first_imag * second_imag
        imag = first_real * second_imag + first_imag * second_real
    out_ref[base : base + rows, :lanes] = imag.astype(bf16)
    out_ref[base : base + rows, lanes:] = real.astype(bf16)


def convolve_kernel(
    pair_ref,
    table_ref,
    twiddle_ref,
    mixed_ref,
    signal_real,
    signal_imag,
    filter_real,
    filter_imag,
    left_ref,
    back_ref,
):
    blocks, rows, lanes = mixed_ref.shape
    height = (blocks + 1) * rows
    first_step(tile_read(pair_ref, 0), twiddle_ref, left_ref, 0, blocks, rows, lanes)
    first_step(tile_read(pair_ref, rows), twiddle_ref, left_ref, height, blocks, rows, lanes)
    spectra = []
    for base, real_ref, imag_ref in (
        (0, signal_real, signal_imag),
        (height, filter_real, filter_imag),
    ):
        spectrum = jnp.dot(
            left_ref[base : base + height], table_ref[...], preferred_element_type=f32
        )
        real_ref[...] = spectrum[:, :lanes].astype(bf16)
        imag_ref[...] = spectrum[:, lanes:].astype(bf16)
        spectra.append(spectrum)
    product(
        spectra[0][:, :lanes],
        spectra[0][:, lanes:],
        spectra[1][:, :lanes],
        spectra[1][:, lanes:],
        left_ref,
        0,
        False,
    )
    back_ref[...] = jnp.dot(left_ref[:height], table_ref[...], preferred_element_type=f32)
    last_step(back_ref, 0, twiddle_ref, tile_write(mixed_ref, 0), blocks, rows, lanes)


def correlate_kernel(
    grad_ref,
    signal_real,
    signal_imag,
    filter_real,
    filter_imag,
    table_ref,
    twiddle_ref,
    out_ref,
    left_ref,
    back_ref,
):
    blocks, rows, lanes = grad_ref.shape
    height = (blocks + 1) * rows
    first_step(tile_read(grad_ref, 0), twiddle_ref, left_ref, 0, blocks, rows, lanes)
    grad = jnp.dot(left_ref[:height], table_ref[...], preferred_element_type=f32)
    for base, real_ref, imag_ref in (
        (0, filter_real, filter_imag),
        (height, signal_real, signal_imag),
    ):
        product(
            grad[:, :lanes],
            grad[:, lanes:],
            real_ref[...].astype(f32),
            imag_ref[...].astype(f32),
            left_ref,
            base,
            True,
        )
    back_ref[...] = jnp.dot(left_ref[...], table_ref[...], preferred_element_type=f32)
    last_step(back_ref, 0, twiddle_ref, tile_write(out_ref, 0), blocks, rows, lanes)
    last_step(back_ref, height, twiddle_ref, tile_write(out_ref, rows), blocks, rows, lanes)


def window_of(decay_ref, length):
    channels = decay_ref.shape[1]
    start = lax.axis_index("seq") * length
    places = (start + lax.broadcasted_iota(jnp.int32, (1, length), 1)).astype(f32)
    rates = jnp.broadcast_to(decay_ref[...], (length, channels)).T
    return jnp.exp(-rates * places) * jnp.sqrt(2.0 * rates)


def send_kernel(decay_in, taps_in, signal_in, pair_ref, decay_ref, taps_ref, signal_ref, sems):
    fetches = [
        pltpu.make_async_copy(source, target, sems.at[at])
        for at, (source, target) in enumerate(
            ((decay_in, decay_ref), (taps_in, taps_ref), (signal_in, signal_ref))
        )
    ]
    for fetch in fetches:
        fetch.start()
    shards, twice, length = pair_ref.shape
    owned = twice // 2
    fetches[0].wait()
    window = window_of(decay_ref, length)
    fetches[1].wait()
    fetches[2].wait()
    filters = (taps_ref[...] * window).astype(bf16)
    for shard in range(shards):
        rows = slice(shard * owned, (shard + 1) * owned)
        pair_ref[shard, :owned] = signal_ref[rows]
        pair_ref[shard, owned:] = filters[rows]


def window_kernel(decay_ref, window_ref):
    window_ref[...] = window_of(decay_ref, window_ref.shape[1])


def spread_kernel(weight_ref, grad_ref, *out_refs):
    count = len(out_refs)
    rows = weight_ref.shape[0] // count
    me = lax.axis_index("chan")
    for step in list(range(1, count)) + [0]:
        place = lax.rem(me + step, count)
        block = weight_ref[pl.ds(pl.multiple_of(place * rows, rows), rows), :]
        out_refs[step][...] = lax.dot_general(
            block, grad_ref[...], (((1,), (1,)), ((), ())), preferred_element_type=f32
        ).astype(out_refs[step].dtype)


def total_kernel(gating_ref, *refs):
    total_ref, grad_mixed_ref = refs[-2:]
    total = refs[0][...].astype(f32)
    for share in refs[1:-2]:
        total = total + share[...].astype(f32)
    total_ref[...] = total.astype(bf16)
    grad_mixed_ref[...] = (total * gating_ref[...].astype(f32)).astype(bf16)


def pack_kernel(both_ref, *out_refs):
    me = lax.axis_index("seq")
    core = lax.rem(me, 2)
    chip = lax.div(me, 2)
    for step, out_ref in enumerate(out_refs):
        block = 2 * lax.bitwise_xor(chip, step) + core
        for source in range(2):
            out_ref[source] = both_ref[source, block]


def mixed_rows(pieces, channels):
    chip = lax.div(lax.axis_index("seq"), 2)
    count = channels // len(pieces)
    for step, piece in enumerate(pieces):
        place = lax.bitwise_xor(chip, step) if len(pieces) > 1 else 0
        rows = pl.ds(pl.multiple_of(place * count, count), count)
        yield rows, piece[...].reshape(count, -1).astype(f32)


def gate_kernel(gating_ref, *refs):
    for rows, mixed in mixed_rows(refs[:-1], gating_ref.shape[0]):
        refs[-1][rows] = (gating_ref[rows].astype(f32) * mixed).astype(bf16)


def gating_grad_kernel(total_ref, *refs):
    for rows, mixed in mixed_rows(refs[:-1], total_ref.shape[0]):
        refs[-1][rows] = total_ref[rows].astype(f32) * mixed


def project_kernel(weight_ref, *refs):
    gated_refs, (out_ref, token_ref) = refs[:-2], refs[-2:]
    token_ref[...] = jnp.zeros_like(token_ref)
    count = len(gated_refs)
    rows = weight_ref.shape[0] // count
    me = lax.axis_index("chan")
    total = None
    for step in range(count):
        place = lax.rem(me + count - step, count)
        block = weight_ref[pl.ds(pl.multiple_of(place * rows, rows), rows), :]
        term = lax.dot_general(
            gated_refs[step][...], block, (((0,), (0,)), ((), ())), preferred_element_type=f32
        )
        total = term if total is None else total + term
    out_ref[...] = total.astype(out_ref.dtype)


def return_kernel(window_ref, *refs):
    pieces, (signal_ref, taps_ref) = refs[:-2], refs[-2:]
    chip = lax.div(lax.axis_index("seq"), 2)
    for step, piece in enumerate(pieces):
        blocks, twice, _ = piece.shape
        owned = twice // 2
        place = lax.bitwise_xor(chip, step) if len(pieces) > 1 else 0
        for source in range(blocks):
            first = pl.multiple_of((place * blocks + source) * owned, owned)
            rows = pl.ds(first, owned)
            signal_ref[rows] = piece[source, :owned].astype(f32)
            taps_ref[rows] = piece[source, owned:].astype(f32) * window_ref[rows]


def padded(array, owned, held):
    if owned == held:
        return array
    blocks, rows, lanes = array.shape
    groups = array.reshape(blocks, rows // owned, owned, lanes)
    groups = jnp.pad(groups, ((0, 0), (0, 0), (0, held - owned), (0, 0)))
    return groups.reshape(blocks, -1, lanes)


def trimmed(array, owned, held):
    if owned == held:
        return array
    blocks, rows, lanes = array.shape
    return array.reshape(blocks, rows // held, held, lanes)[:, :, :owned].reshape(blocks, -1, lanes)


def exchange(array):
    return lax.all_to_all(array, "seq", split_axis=0, concat_axis=0, tiled=True)


def per_device(signal, gating, filter_taps, decay_rates, out_weight, out_grad):
    channels, length = signal.shape
    shards = lax.axis_size("seq")
    parts = lax.axis_size("chan")
    owned = channels // shards
    held = -(-owned // ROWS) * ROWS
    height = (shards + 1) * held
    table = jnp.asarray(within_table(length))
    twiddle = jnp.asarray(twiddle_table(shards, length))
    shape = jax.ShapeDtypeStruct

    def shift(array, step):
        return lax.ppermute(array, "chan", [(i, (i + step) % parts) for i in range(parts)])

    rates = decay_rates.reshape(1, channels)
    if owned == held:
        pairs = call(
            send_kernel,
            shape((shards, 2 * owned, length), bf16),
            [ANY] * 3,
            (
                pltpu.VMEM((1, channels), f32),
                pltpu.VMEM((channels, length), f32),
                pltpu.VMEM((channels, length), bf16),
                pltpu.SemaphoreType.DMA((3,)),
            ),
            room=62,
        )(rates, filter_taps, signal)
    else:
        pairs = send_plain(decay_rates, filter_taps, signal, shards)
    arrived = exchange(pairs)

    partial = call(
        spread_kernel,
        tuple(shape((channels, length), bf16) for k in range(parts)),
        [VMEM] * 2,
        after=(pairs,),
    )(out_weight, out_grad)
    shares = [shift(partial[step], step) for step in range(1, parts)]

    mixed_owned, *spectra = call(
        convolve_kernel,
        (shape((shards, held, length), bf16),) + 4 * (shape((height, length), bf16),),
        [VMEM] * 3,
        (
            pltpu.VMEM((2 * height, 2 * length), bf16),
            pltpu.VMEM((height, 2 * length), f32),
        ),
        micros=2,
    )(padded(arrived, owned, held), table, twiddle)
    chips = shards // 2
    direct = chips in (2, 4) and owned == held

    def hop(array, distance):
        return lax.ppermute(array, "seq", [(i, i ^ distance) for i in range(shards)])

    def bring(array):
        if not direct:
            return [exchange(array)]
        pairs = [[2 * chip, 2 * chip + 1] for chip in range(chips)]
        both = lax.all_gather(array, "seq", axis_index_groups=pairs)
        packed = call(
            pack_kernel, (shape((2,) + array.shape[1:], bf16),) * chips, [VMEM], micros=0
        )(both)
        return [packed[0]] + [hop(packed[step], 2 * step) for step in range(1, chips)]

    pieces = bring(trimmed(mixed_owned, owned, held))

    total, grad_mixed = call(
        total_kernel,
        (shape((channels, length), bf16),) * 2,
        [VMEM] * (2 + len(shares)),
        after=(pieces[0],),
    )(gating, partial[0], *shares)
    grad_whole = exchange(grad_mixed.reshape(shards, owned, length))

    gated = call(gate_kernel, shape((channels, length), bf16), [VMEM] * (1 + len(pieces)))(
        gating, *pieces
    )
    gathered = [gated] + [shift(gated, step) for step in range(1, parts)]
    mixed_out, projected = call(
        project_kernel,
        (shape((length, out_weight.shape[1]), bf16), shape((8, LANES), f32)),
        [VMEM] * (1 + parts),
        micros=12.0,
    )(out_weight, *gathered)

    grads_owned = call(
        correlate_kernel,
        shape((shards, 2 * held, length), bf16),
        [VMEM] * 7,
        (
            pltpu.VMEM((2 * height, 2 * length), bf16),
            pltpu.VMEM((2 * height, 2 * length), f32),
        ),
        micros=2.0,
        after=(gated,),
    )(padded(grad_whole, owned, held), *spectra, table, twiddle)
    returned = bring(trimmed(grads_owned, owned, held))
    gating_grad = call(
        gating_grad_kernel, shape((channels, length), f32), [VMEM] * (1 + len(pieces)), after=(projected,)
    )(total, *pieces)
    window = call(window_kernel, shape((channels, length), f32), [VMEM], after=(projected,))(rates)
    if owned == held:
        signal_grad, taps_grad = call(
            return_kernel,
            (shape((channels, length), f32), shape((channels, length), f32)),
            [VMEM] * (1 + len(returned)),
        )(window, *returned)
    else:
        both = returned[0].reshape(shards, 2, owned, length).astype(f32)
        signal_grad = both[:, 0].reshape(channels, length)
        taps_grad = both[:, 1].reshape(channels, length) * window
    return (mixed_out, signal_grad, gating_grad, taps_grad)


def send_plain(decay_rates, filter_taps, signal, shards):
    channels, length = signal.shape
    owned = channels // shards
    places = (lax.axis_index("seq") * length + jnp.arange(length, dtype=jnp.int32)).astype(f32)
    rates = decay_rates[:, None]
    window = jnp.exp(-rates * places[None, :]) * jnp.sqrt(2.0 * rates)
    filters = (filter_taps * window).astype(bf16)
    pairs = jnp.stack([part.reshape(shards, owned, length) for part in (signal, filters)], 1)
    return pairs.reshape(shards, 2 * owned, length)


def solution(mesh):
    in_specs = (
        P("chan", "seq"),
        P("chan", "seq"),
        P("chan", "seq"),
        P("chan"),
        P(None, "chan"),
        P("seq", "chan"),
    )
    out_specs = (P("seq", "chan"), P("chan", "seq"), P("chan", "seq"), P("chan", "seq"))
    return jax.shard_map(
        per_device, mesh=mesh, in_specs=in_specs, out_specs=out_specs, check_vma=False
    )
```

```python
import functools

import jax
import jax.numpy as jnp
import ml_dtypes
import numpy as np
from jax import lax
from jax.experimental import pallas as pl
from jax.experimental.pallas import tpu as pltpu
from jax.sharding import PartitionSpec as P

f32 = jnp.float32
bf16 = jnp.bfloat16
VMEM = pl.BlockSpec(memory_space=pltpu.VMEM)
ANY = pl.BlockSpec(memory_space=pl.ANY)
PEAK_FLOPS_A_MICRO = 1.15e9
ROWS = 16
LANES = 128


def call(kernel, out_shape, in_specs, scratch=(), micros=1, room=16, after=()):
    count = len(in_specs)

    def body(*refs):
        kernel(*refs[:count], *refs[count + len(after) :])

    run = pl.pallas_call(
        body,
        out_shape=out_shape,
        in_specs=list(in_specs) + [ANY] * len(after),
        out_specs=jax.tree.map(lambda _: VMEM, out_shape),
        scratch_shapes=list(scratch),
        cost_estimate=pl.CostEstimate(
            flops=int(micros * PEAK_FLOPS_A_MICRO), bytes_accessed=0, transcendentals=0
        ),
        compiler_params=pltpu.CompilerParams(vmem_limit_bytes=room * 1024 * 1024),
    )
    return lambda *operands: run(*operands, *after)


def within_table(lanes):
    index = np.arange(lanes)
    angle = 2.0 * np.pi * (np.outer(index, index) % lanes) / lanes
    cos, sin = np.cos(angle), np.sin(angle)
    table = np.concatenate(
        [np.concatenate([cos, -sin], 1), np.concatenate([sin, cos], 1)], 0
    )
    return table.astype(ml_dtypes.bfloat16)


def twiddle_table(blocks, lanes):
    rows = np.arange(blocks + 1)[:, None]
    angle = 2.0 * np.pi * rows * np.arange(lanes)[None, :] / (2 * blocks * lanes)
    return np.stack([np.cos(angle), np.sin(angle)], 1).astype(np.float32)


def turned(real, imag, turn, size):
    angle = 2.0 * np.pi * turn / size
    cos, sin = float(np.cos(angle)), float(np.sin(angle))
    if turn == 0:
        return real, imag
    if abs(abs(cos) - abs(sin)) < 1e-9:
        root = abs(cos)
        cs, ss = (1 if cos > 0 else -1), (1 if sin > 0 else -1)
        first = real if cs > 0 else -real
        if cs == ss:
            return (root * cs) * (real - imag), (root * cs) * (real + imag)
        return (root * cs) * (real + imag), (root * cs) * (imag - real)
    return cos * real - sin * imag, sin * real + cos * imag


def real_forward(tiles, size):
    if size == 2:
        return [(tiles[0], None), (tiles[0], None)]
    even = real_forward(tiles[0::2], size // 2)
    odd = real_forward(tiles[1::2], size // 2)
    quarter = size // 4
    out = [None] * (size // 2 + 1)
    out[0] = (even[0][0] + odd[0][0], None)
    out[size // 2] = (even[0][0] - odd[0][0], None)
    for row in range(1, quarter):
        real, imag = turned(odd[row][0], odd[row][1], -row, size)
        out[row] = (even[row][0] + real, even[row][1] + imag)
        out[size // 2 - row] = (even[row][0] - real, imag - even[row][1])
    out[quarter] = (even[quarter][0], -odd[quarter][0])
    return out


def real_inverse(rows, size):
    if size == 2:
        return [rows[0][0] + rows[1][0]]
    quarter = size // 4
    even, odd = [], []
    for row in range(quarter + 1):
        real, imag = rows[row]
        if row == 0:
            last = rows[size // 2][0]
            even.append((real + last, None))
            odd.append((real - last, None))
        elif row == quarter:
            even.append((2.0 * real, None))
            odd.append((-2.0 * imag, None))
        else:
            far_real, far_imag = rows[size // 2 - row]
            even.append((real + far_real, imag - far_imag))
            odd.append(turned(real - far_real, imag + far_imag, row, size))
    firsts = real_inverse(even, size // 2)
    seconds = real_inverse(odd, size // 2)
    return [tile for pair in zip(firsts, seconds) for tile in pair]


def tile_slices(rows, lanes):
    for row in range(0, rows, ROWS):
        for lane in range(0, lanes, LANES):
            yield row, lane


def first_step(read, twiddle_ref, out_ref, base, blocks, rows, lanes):
    for row, lane in tile_slices(rows, lanes):
        tiles = [read(block, row, lane) for block in range(blocks)]
        for step, (real, imag) in enumerate(real_forward(tiles, 2 * blocks)):
            cos = twiddle_ref[step, 0:1, lane : lane + LANES]
            sin = twiddle_ref[step, 1:2, lane : lane + LANES]
            if step == 0:
                new_real, new_imag = real, jnp.zeros_like(real)
            elif imag is None:
                new_real, new_imag = real * cos, -real * sin
            else:
                new_real, new_imag = real * cos + imag * sin, imag * cos - real * sin
            at = base + step * rows + row
            out_ref[at : at + ROWS, lane : lane + LANES] = new_real.astype(bf16)
            out_ref[at : at + ROWS, lanes + lane : lanes + lane + LANES] = new_imag.astype(bf16)


def last_step(spec_ref, base, twiddle_ref, write, blocks, rows, lanes):
    scale = 1.0 / (2 * blocks * lanes)
    for row, lane in tile_slices(rows, lanes):
        steps = []
        for step in range(blocks + 1):
            at = base + step * rows + row
            imag = spec_ref[at : at + ROWS, lane : lane + LANES]
            real = spec_ref[at : at + ROWS, lanes + lane : lanes + lane + LANES]
            cos = twiddle_ref[step, 0:1, lane : lane + LANES] * scale
            sin = twiddle_ref[step, 1:2, lane : lane + LANES] * scale
            new_real = real * cos - imag * sin
            if step == 0 or step == blocks:
                steps.append((new_real, None))
            else:
                steps.append((new_real, imag * cos + real * sin))
        for block, tile in enumerate(real_inverse(steps, 2 * blocks)):
            write(block, row, lane, tile)


def tile_read(ref, base):
    def read(block, row, lane):
        at = base + row
        return ref[block, at : at + ROWS, lane : lane + LANES].astype(f32)

    return read


def tile_write(ref, base):
    def write(block, row, lane, tile):
        at = base + row
        ref[block, at : at + ROWS, lane : lane + LANES] = tile.astype(ref.dtype)

    return write


def product(first_real, first_imag, second_real, second_imag, out_ref, base, conjugate):
    rows, lanes = first_real.shape
    if conjugate:
        real = first_real * second_real + first_imag * second_imag
        imag = first_imag * second_real - first_real * second_imag
    else:
        real = first_real * second_real - first_imag * second_imag
        imag = first_real * second_imag + first_imag * second_real
    out_ref[base : base + rows, :lanes] = imag.astype(bf16)
    out_ref[base : base + rows, lanes:] = real.astype(bf16)


def convolve_kernel(
    pair_ref,
    table_ref,
    twiddle_ref,
    mixed_ref,
    signal_real,
    signal_imag,
    filter_real,
    filter_imag,
    left_ref,
    back_ref,
):
    blocks, rows, lanes = mixed_ref.shape
    height = (blocks + 1) * rows
    first_step(tile_read(pair_ref, 0), twiddle_ref, left_ref, 0, blocks, rows, lanes)
    first_step(tile_read(pair_ref, rows), twiddle_ref, left_ref, height, blocks, rows, lanes)
    spectra = []
    for base, real_ref, imag_ref in (
        (0, signal_real, signal_imag),
        (height, filter_real, filter_imag),
    ):
        spectrum = jnp.dot(
            left_ref[base : base + height], table_ref[...], preferred_element_type=f32
        )
        real_ref[...] = spectrum[:, :lanes].astype(bf16)
        imag_ref[...] = spectrum[:, lanes:].astype(bf16)
        spectra.append(spectrum)
    product(
        spectra[0][:, :lanes],
        spectra[0][:, lanes:],
        spectra[1][:, :lanes],
        spectra[1][:, lanes:],
        left_ref,
        0,
        False,
    )
    back_ref[...] = jnp.dot(left_ref[:height], table_ref[...], preferred_element_type=f32)
    last_step(back_ref, 0, twiddle_ref, tile_write(mixed_ref, 0), blocks, rows, lanes)


def correlate_kernel(
    grad_ref,
    signal_real,
    signal_imag,
    filter_real,
    filter_imag,
    table_ref,
    twiddle_ref,
    out_ref,
    left_ref,
    back_ref,
):
    blocks, rows, lanes = grad_ref.shape
    height = (blocks + 1) * rows
    first_step(tile_read(grad_ref, 0), twiddle_ref, left_ref, 0, blocks, rows, lanes)
    grad = jnp.dot(left_ref[:height], table_ref[...], preferred_element_type=f32)
    for base, real_ref, imag_ref in (
        (0, filter_real, filter_imag),
        (height, signal_real, signal_imag),
    ):
        product(
            grad[:, :lanes],
            grad[:, lanes:],
            real_ref[...].astype(f32),
            imag_ref[...].astype(f32),
            left_ref,
            base,
            True,
        )
    back_ref[...] = jnp.dot(left_ref[...], table_ref[...], preferred_element_type=f32)
    last_step(back_ref, 0, twiddle_ref, tile_write(out_ref, 0), blocks, rows, lanes)
    last_step(back_ref, height, twiddle_ref, tile_write(out_ref, rows), blocks, rows, lanes)


def window_of(decay_ref, length):
    channels = decay_ref.shape[1]
    start = lax.axis_index("seq") * length
    places = (start + lax.broadcasted_iota(jnp.int32, (1, length), 1)).astype(f32)
    rates = jnp.broadcast_to(decay_ref[...], (length, channels)).T
    return jnp.exp(-rates * places) * jnp.sqrt(2.0 * rates)


def send_kernel(decay_in, taps_in, signal_in, pair_ref, decay_ref, taps_ref, signal_ref, sems):
    fetches = [
        pltpu.make_async_copy(source, target, sems.at[at])
        for at, (source, target) in enumerate(
            ((decay_in, decay_ref), (taps_in, taps_ref), (signal_in, signal_ref))
        )
    ]
    for fetch in fetches:
        fetch.start()
    shards, twice, length = pair_ref.shape
    owned = twice // 2
    fetches[0].wait()
    window = window_of(decay_ref, length)
    fetches[1].wait()
    fetches[2].wait()
    filters = (taps_ref[...] * window).astype(bf16)
    for shard in range(shards):
        rows = slice(shard * owned, (shard + 1) * owned)
        pair_ref[shard, :owned] = signal_ref[rows]
        pair_ref[shard, owned:] = filters[rows]


def spread_kernel(weight_ref, grad_ref, *out_refs):
    count = len(out_refs)
    rows = weight_ref.shape[0] // count
    me = lax.axis_index("chan")
    for step in list(range(1, count)) + [0]:
        place = lax.rem(me + step, count)
        block = weight_ref[pl.ds(pl.multiple_of(place * rows, rows), rows), :]
        out_refs[step][...] = lax.dot_general(
            block, grad_ref[...], (((1,), (1,)), ((), ())), preferred_element_type=f32
        ).astype(out_refs[step].dtype)


def total_kernel(gating_ref, *refs):
    total_ref, grad_mixed_ref = refs[-2:]
    total = refs[0][...].astype(f32)
    for share in refs[1:-2]:
        total = total + share[...].astype(f32)
    total_ref[...] = total.astype(bf16)
    grad_mixed_ref[...] = (total * gating_ref[...].astype(f32)).astype(bf16)


def pack_kernel(both_ref, *out_refs):
    me = lax.axis_index("seq")
    core = lax.rem(me, 2)
    chip = lax.div(me, 2)
    for step, out_ref in enumerate(out_refs):
        block = 2 * lax.bitwise_xor(chip, step) + core
        for source in range(2):
            out_ref[source] = both_ref[source, block]


def mixed_rows(pieces, channels):
    chip = lax.div(lax.axis_index("seq"), 2)
    count = channels // len(pieces)
    for step, piece in enumerate(pieces):
        place = lax.bitwise_xor(chip, step) if len(pieces) > 1 else 0
        rows = pl.ds(pl.multiple_of(place * count, count), count)
        yield rows, piece[...].reshape(count, -1).astype(f32)


def gate_kernel(gating_ref, *refs):
    for rows, mixed in mixed_rows(refs[:-1], gating_ref.shape[0]):
        refs[-1][rows] = (gating_ref[rows].astype(f32) * mixed).astype(bf16)


def project_kernel(count, weight_ref, total_ref, decay_ref, *refs):
    gated_refs, pieces = refs[:count], refs[count:-3]
    out_ref, gating_grad_ref, window_ref = refs[-3:]
    window_ref[...] = window_of(decay_ref, total_ref.shape[1])
    for rows, mixed in mixed_rows(pieces, total_ref.shape[0]):
        gating_grad_ref[rows] = total_ref[rows].astype(f32) * mixed
    rows = weight_ref.shape[0] // count
    me = lax.axis_index("chan")
    total = None
    for step in range(count):
        place = lax.rem(me + count - step, count)
        block = weight_ref[pl.ds(pl.multiple_of(place * rows, rows), rows), :]
        term = lax.dot_general(
            gated_refs[step][...], block, (((0,), (0,)), ((), ())), preferred_element_type=f32
        )
        total = term if total is None else total + term
    out_ref[...] = total.astype(out_ref.dtype)


def return_kernel(order, window_ref, *refs):
    pieces, (signal_ref, taps_ref) = refs[:-2], refs[-2:]
    chip = lax.div(lax.axis_index("seq"), 2)
    for step, piece in zip(order, pieces):
        blocks, twice, _ = piece.shape
        owned = twice // 2
        place = lax.bitwise_xor(chip, step) if len(pieces) > 1 else 0
        for source in range(blocks):
            first = pl.multiple_of((place * blocks + source) * owned, owned)
            rows = pl.ds(first, owned)
            signal_ref[rows] = piece[source, :owned].astype(f32)
            taps_ref[rows] = piece[source, owned:].astype(f32) * window_ref[rows]


def padded(array, owned, held):
    if owned == held:
        return array
    blocks, rows, lanes = array.shape
    groups = array.reshape(blocks, rows // owned, owned, lanes)
    groups = jnp.pad(groups, ((0, 0), (0, 0), (0, held - owned), (0, 0)))
    return groups.reshape(blocks, -1, lanes)


def trimmed(array, owned, held):
    if owned == held:
        return array
    blocks, rows, lanes = array.shape
    return array.reshape(blocks, rows // held, held, lanes)[:, :, :owned].reshape(blocks, -1, lanes)


def exchange(array):
    return lax.all_to_all(array, "seq", split_axis=0, concat_axis=0, tiled=True)


def per_device(signal, gating, filter_taps, decay_rates, out_weight, out_grad):
    channels, length = signal.shape
    shards = lax.axis_size("seq")
    parts = lax.axis_size("chan")
    owned = channels // shards
    held = -(-owned // ROWS) * ROWS
    height = (shards + 1) * held
    table = jnp.asarray(within_table(length))
    twiddle = jnp.asarray(twiddle_table(shards, length))
    shape = jax.ShapeDtypeStruct

    def shift(array, step):
        return lax.ppermute(array, "chan", [(i, (i + step) % parts) for i in range(parts)])

    rates = decay_rates.reshape(1, channels)
    if owned == held:
        pairs = call(
            send_kernel,
            shape((shards, 2 * owned, length), bf16),
            [ANY] * 3,
            (
                pltpu.VMEM((1, channels), f32),
                pltpu.VMEM((channels, length), f32),
                pltpu.VMEM((channels, length), bf16),
                pltpu.SemaphoreType.DMA((3,)),
            ),
            room=62,
        )(rates, filter_taps, signal)
    else:
        pairs = send_plain(decay_rates, filter_taps, signal, shards)
    arrived = exchange(pairs)

    partial = call(
        spread_kernel,
        tuple(shape((channels, length), bf16) for k in range(parts)),
        [VMEM] * 2,
        after=(pairs,),
    )(out_weight, out_grad)
    shares = [shift(partial[step], step) for step in range(1, parts)]

    mixed_owned, *spectra = call(
        convolve_kernel,
        (shape((shards, held, length), bf16),) + 4 * (shape((height, length), bf16),),
        [VMEM] * 3,
        (
            pltpu.VMEM((2 * height, 2 * length), bf16),
            pltpu.VMEM((height, 2 * length), f32),
        ),
        micros=2,
    )(padded(arrived, owned, held), table, twiddle)
    chips = shards // 2
    direct = chips in (2, 4) and owned == held

    def hop(array, distance):
        return lax.ppermute(array, "seq", [(i, i ^ distance) for i in range(shards)])

    def bring(array):
        if not direct:
            return [exchange(array)]
        pairs = [[2 * chip, 2 * chip + 1] for chip in range(chips)]
        both = lax.all_gather(array, "seq", axis_index_groups=pairs)
        packed = call(
            pack_kernel, (shape((2,) + array.shape[1:], bf16),) * chips, [VMEM], micros=0
        )(both)
        return [packed[0]] + [hop(packed[step], 2 * step) for step in range(1, chips)]

    pieces = bring(trimmed(mixed_owned, owned, held))

    total, grad_mixed = call(
        total_kernel,
        (shape((channels, length), bf16),) * 2,
        [VMEM] * (2 + len(shares)),
        after=(pieces[0],),
    )(gating, partial[0], *shares)
    grad_whole = exchange(grad_mixed.reshape(shards, owned, length))

    gated = call(gate_kernel, shape((channels, length), bf16), [VMEM] * (1 + len(pieces)))(
        gating, *pieces
    )
    gathered = [gated] + [shift(gated, step) for step in range(1, parts)]
    mixed_out, gating_grad, window = call(
        functools.partial(project_kernel, parts),
        (
            shape((length, out_weight.shape[1]), bf16),
            shape((channels, length), f32),
            shape((channels, length), f32),
        ),
        [VMEM] * (3 + parts + len(pieces)),
        micros=12.0,
    )(out_weight, total, rates, *gathered, *pieces)

    grads_owned = call(
        correlate_kernel,
        shape((shards, 2 * held, length), bf16),
        [VMEM] * 7,
        (
            pltpu.VMEM((2 * height, 2 * length), bf16),
            pltpu.VMEM((2 * height, 2 * length), f32),
        ),
        micros=2.0,
        after=(gated,),
    )(padded(grad_whole, owned, held), *spectra, table, twiddle)
    returned = bring(trimmed(grads_owned, owned, held))
    order = (0, 2, 3, 1) if len(returned) == 4 else range(len(returned))
    if owned == held:
        signal_grad, taps_grad = call(
            functools.partial(return_kernel, order),
            (shape((channels, length), f32), shape((channels, length), f32)),
            [VMEM] * (1 + len(returned)),
        )(window, *(returned[step] for step in order))
    else:
        both = returned[0].reshape(shards, 2, owned, length).astype(f32)
        signal_grad = both[:, 0].reshape(channels, length)
        taps_grad = both[:, 1].reshape(channels, length) * window
    return (mixed_out, signal_grad, gating_grad, taps_grad)


def send_plain(decay_rates, filter_taps, signal, shards):
    channels, length = signal.shape
    owned = channels // shards
    places = (lax.axis_index("seq") * length + jnp.arange(length, dtype=jnp.int32)).astype(f32)
    rates = decay_rates[:, None]
    window = jnp.exp(-rates * places[None, :]) * jnp.sqrt(2.0 * rates)
    filters = (filter_taps * window).astype(bf16)
    pairs = jnp.stack([part.reshape(shards, owned, length) for part in (signal, filters)], 1)
    return pairs.reshape(shards, 2 * owned, length)


def solution(mesh):
    in_specs = (
        P("chan", "seq"),
        P("chan", "seq"),
        P("chan", "seq"),
        P("chan"),
        P(None, "chan"),
        P("seq", "chan"),
    )
    out_specs = (P("seq", "chan"), P("chan", "seq"), P("chan", "seq"), P("chan", "seq"))
    return jax.shard_map(
        per_device, mesh=mesh, in_specs=in_specs, out_specs=out_specs, check_vma=False
    )
```

```python
import functools

import jax
import jax.numpy as jnp
import ml_dtypes
import numpy as np
from jax import lax
from jax.experimental import pallas as pl
from jax.experimental.pallas import tpu as pltpu
from jax.sharding import PartitionSpec as P

f32 = jnp.float32
bf16 = jnp.bfloat16
VMEM = pl.BlockSpec(memory_space=pltpu.VMEM)
ANY = pl.BlockSpec(memory_space=pl.ANY)
PEAK_FLOPS_A_MICRO = 1.15e9
ROWS = 16
LANES = 128


def call(kernel, out_shape, in_specs, scratch=(), micros=1, room=16, after=()):
    count = len(in_specs)

    def body(*refs):
        kernel(*refs[:count], *refs[count + len(after) :])

    run = pl.pallas_call(
        body,
        out_shape=out_shape,
        in_specs=list(in_specs) + [ANY] * len(after),
        out_specs=jax.tree.map(lambda _: VMEM, out_shape),
        scratch_shapes=list(scratch),
        cost_estimate=pl.CostEstimate(
            flops=int(micros * PEAK_FLOPS_A_MICRO), bytes_accessed=0, transcendentals=0
        ),
        compiler_params=pltpu.CompilerParams(vmem_limit_bytes=room * 1024 * 1024),
    )
    return lambda *operands: run(*operands, *after)


def within_table(lanes):
    index = np.arange(lanes)
    angle = 2.0 * np.pi * (np.outer(index, index) % lanes) / lanes
    cos, sin = np.cos(angle), np.sin(angle)
    table = np.concatenate(
        [np.concatenate([cos, -sin], 1), np.concatenate([sin, cos], 1)], 0
    )
    return table.astype(ml_dtypes.bfloat16)


def twiddle_table(blocks, lanes):
    rows = np.arange(blocks + 1)[:, None]
    angle = 2.0 * np.pi * rows * np.arange(lanes)[None, :] / (2 * blocks * lanes)
    return np.stack([np.cos(angle), np.sin(angle)], 1).astype(np.float32)


def turned(real, imag, turn, size):
    angle = 2.0 * np.pi * turn / size
    cos, sin = float(np.cos(angle)), float(np.sin(angle))
    if turn == 0:
        return real, imag
    if abs(abs(cos) - abs(sin)) < 1e-9:
        root = abs(cos)
        cs, ss = (1 if cos > 0 else -1), (1 if sin > 0 else -1)
        first = real if cs > 0 else -real
        if cs == ss:
            return (root * cs) * (real - imag), (root * cs) * (real + imag)
        return (root * cs) * (real + imag), (root * cs) * (imag - real)
    return cos * real - sin * imag, sin * real + cos * imag


def real_forward(tiles, size):
    if size == 2:
        return [(tiles[0], None), (tiles[0], None)]
    even = real_forward(tiles[0::2], size // 2)
    odd = real_forward(tiles[1::2], size // 2)
    quarter = size // 4
    out = [None] * (size // 2 + 1)
    out[0] = (even[0][0] + odd[0][0], None)
    out[size // 2] = (even[0][0] - odd[0][0], None)
    for row in range(1, quarter):
        real, imag = turned(odd[row][0], odd[row][1], -row, size)
        out[row] = (even[row][0] + real, even[row][1] + imag)
        out[size // 2 - row] = (even[row][0] - real, imag - even[row][1])
    out[quarter] = (even[quarter][0], -odd[quarter][0])
    return out


def real_inverse(rows, size):
    if size == 2:
        return [rows[0][0] + rows[1][0]]
    quarter = size // 4
    even, odd = [], []
    for row in range(quarter + 1):
        real, imag = rows[row]
        if row == 0:
            last = rows[size // 2][0]
            even.append((real + last, None))
            odd.append((real - last, None))
        elif row == quarter:
            even.append((2.0 * real, None))
            odd.append((-2.0 * imag, None))
        else:
            far_real, far_imag = rows[size // 2 - row]
            even.append((real + far_real, imag - far_imag))
            odd.append(turned(real - far_real, imag + far_imag, row, size))
    firsts = real_inverse(even, size // 2)
    seconds = real_inverse(odd, size // 2)
    return [tile for pair in zip(firsts, seconds) for tile in pair]


def tile_slices(rows, lanes):
    for row in range(0, rows, ROWS):
        for lane in range(0, lanes, LANES):
            yield row, lane


def first_step(read, twiddle_ref, out_ref, base, blocks, rows, lanes):
    for row, lane in tile_slices(rows, lanes):
        tiles = [read(block, row, lane) for block in range(blocks)]
        for step, (real, imag) in enumerate(real_forward(tiles, 2 * blocks)):
            cos = twiddle_ref[step, 0:1, lane : lane + LANES]
            sin = twiddle_ref[step, 1:2, lane : lane + LANES]
            if step == 0:
                new_real, new_imag = real, jnp.zeros_like(real)
            elif imag is None:
                new_real, new_imag = real * cos, -real * sin
            else:
                new_real, new_imag = real * cos + imag * sin, imag * cos - real * sin
            at = base + step * rows + row
            out_ref[at : at + ROWS, lane : lane + LANES] = new_real.astype(bf16)
            out_ref[at : at + ROWS, lanes + lane : lanes + lane + LANES] = new_imag.astype(bf16)


def last_step(spec_ref, base, twiddle_ref, write, blocks, rows, lanes):
    scale = 1.0 / (2 * blocks * lanes)
    for row, lane in tile_slices(rows, lanes):
        steps = []
        for step in range(blocks + 1):
            at = base + step * rows + row
            imag = spec_ref[at : at + ROWS, lane : lane + LANES]
            real = spec_ref[at : at + ROWS, lanes + lane : lanes + lane + LANES]
            cos = twiddle_ref[step, 0:1, lane : lane + LANES] * scale
            sin = twiddle_ref[step, 1:2, lane : lane + LANES] * scale
            new_real = real * cos - imag * sin
            if step == 0 or step == blocks:
                steps.append((new_real, None))
            else:
                steps.append((new_real, imag * cos + real * sin))
        for block, tile in enumerate(real_inverse(steps, 2 * blocks)):
            write(block, row, lane, tile)


def tile_read(ref, base):
    def read(block, row, lane):
        at = base + row
        return ref[block, at : at + ROWS, lane : lane + LANES].astype(f32)

    return read


def tile_write(ref, base):
    def write(block, row, lane, tile):
        at = base + row
        ref[block, at : at + ROWS, lane : lane + LANES] = tile.astype(ref.dtype)

    return write


def product(first_real, first_imag, second_real, second_imag, out_ref, base, conjugate):
    rows, lanes = first_real.shape
    if conjugate:
        real = first_real * second_real + first_imag * second_imag
        imag = first_imag * second_real - first_real * second_imag
    else:
        real = first_real * second_real - first_imag * second_imag
        imag = first_real * second_imag + first_imag * second_real
    out_ref[base : base + rows, :lanes] = imag.astype(bf16)
    out_ref[base : base + rows, lanes:] = real.astype(bf16)


def convolve_kernel(
    pair_ref,
    table_ref,
    twiddle_ref,
    mixed_ref,
    signal_real,
    signal_imag,
    filter_real,
    filter_imag,
    left_ref,
    back_ref,
):
    blocks, rows, lanes = mixed_ref.shape
    height = (blocks + 1) * rows
    first_step(tile_read(pair_ref, 0), twiddle_ref, left_ref, 0, blocks, rows, lanes)
    first_step(tile_read(pair_ref, rows), twiddle_ref, left_ref, height, blocks, rows, lanes)
    spectra = []
    for base, real_ref, imag_ref in (
        (0, signal_real, signal_imag),
        (height, filter_real, filter_imag),
    ):
        spectrum = jnp.dot(
            left_ref[base : base + height], table_ref[...], preferred_element_type=f32
        )
        real_ref[...] = spectrum[:, :lanes].astype(bf16)
        imag_ref[...] = spectrum[:, lanes:].astype(bf16)
        spectra.append(spectrum)
    product(
        spectra[0][:, :lanes],
        spectra[0][:, lanes:],
        spectra[1][:, :lanes],
        spectra[1][:, lanes:],
        left_ref,
        0,
        False,
    )
    back_ref[...] = jnp.dot(left_ref[:height], table_ref[...], preferred_element_type=f32)
    last_step(back_ref, 0, twiddle_ref, tile_write(mixed_ref, 0), blocks, rows, lanes)


def correlate_kernel(
    grad_ref,
    signal_real,
    signal_imag,
    filter_real,
    filter_imag,
    table_ref,
    twiddle_ref,
    out_ref,
    left_ref,
    back_ref,
):
    blocks, rows, lanes = grad_ref.shape
    height = (blocks + 1) * rows
    first_step(tile_read(grad_ref, 0), twiddle_ref, left_ref, 0, blocks, rows, lanes)
    grad = jnp.dot(left_ref[:height], table_ref[...], preferred_element_type=f32)
    for base, real_ref, imag_ref in (
        (0, filter_real, filter_imag),
        (height, signal_real, signal_imag),
    ):
        product(
            grad[:, :lanes],
            grad[:, lanes:],
            real_ref[...].astype(f32),
            imag_ref[...].astype(f32),
            left_ref,
            base,
            True,
        )
    back_ref[...] = jnp.dot(left_ref[...], table_ref[...], preferred_element_type=f32)
    last_step(back_ref, 0, twiddle_ref, tile_write(out_ref, 0), blocks, rows, lanes)
    last_step(back_ref, height, twiddle_ref, tile_write(out_ref, rows), blocks, rows, lanes)


def window_of(decay_ref, length):
    channels = decay_ref.shape[1]
    start = lax.axis_index("seq") * length
    places = (start + lax.broadcasted_iota(jnp.int32, (1, length), 1)).astype(f32)
    rates = jnp.broadcast_to(decay_ref[...], (length, channels)).T
    return jnp.exp(-rates * places) * jnp.sqrt(2.0 * rates)


def send_kernel(decay_in, taps_in, signal_in, pair_ref, decay_ref, taps_ref, signal_ref, sems):
    fetches = [
        pltpu.make_async_copy(source, target, sems.at[at])
        for at, (source, target) in enumerate(
            ((decay_in, decay_ref), (taps_in, taps_ref), (signal_in, signal_ref))
        )
    ]
    for fetch in fetches:
        fetch.start()
    shards, twice, length = pair_ref.shape
    owned = twice // 2
    fetches[0].wait()
    window = window_of(decay_ref, length)
    fetches[1].wait()
    fetches[2].wait()
    filters = (taps_ref[...] * window).astype(bf16)
    for shard in range(shards):
        rows = slice(shard * owned, (shard + 1) * owned)
        pair_ref[shard, :owned] = signal_ref[rows]
        pair_ref[shard, owned:] = filters[rows]


def look_up(table, index):
    value = jnp.int32(table[0])
    for at in range(1, len(table)):
        value = jnp.where(index == at, jnp.int32(table[at]), value)
    return value


def spread_kernel(routes, weight_ref, grad_ref, *out_refs):
    count = len(out_refs)
    rows = weight_ref.shape[0] // count
    me = lax.axis_index("chan")
    for step in list(range(1, count)) + [0]:
        place = look_up(routes[step], me)
        block = weight_ref[pl.ds(pl.multiple_of(place * rows, rows), rows), :]
        out_refs[step][...] = lax.dot_general(
            block, grad_ref[...], (((1,), (1,)), ((), ())), preferred_element_type=f32
        ).astype(out_refs[step].dtype)


def total_kernel(gating_ref, *refs):
    total_ref, grad_mixed_ref = refs[-2:]
    total = refs[0][...].astype(f32)
    for share in refs[1:-2]:
        total = total + share[...].astype(f32)
    total_ref[...] = total.astype(bf16)
    grad_mixed_ref[...] = (total * gating_ref[...].astype(f32)).astype(bf16)


def pack_kernel(both_ref, *out_refs):
    me = lax.axis_index("seq")
    core = lax.rem(me, 2)
    chip = lax.div(me, 2)
    for step, out_ref in enumerate(out_refs):
        block = 2 * lax.bitwise_xor(chip, step) + core
        for source in range(2):
            out_ref[source] = both_ref[source, block]


def mixed_rows(pieces, channels):
    chip = lax.div(lax.axis_index("seq"), 2)
    count = channels // len(pieces)
    for step, piece in enumerate(pieces):
        place = lax.bitwise_xor(chip, step) if len(pieces) > 1 else 0
        rows = pl.ds(pl.multiple_of(place * count, count), count)
        yield rows, piece[...].reshape(count, -1).astype(f32)


def gate_kernel(gating_ref, *refs):
    for rows, mixed in mixed_rows(refs[:-1], gating_ref.shape[0]):
        refs[-1][rows] = (gating_ref[rows].astype(f32) * mixed).astype(bf16)


def project_kernel(routes, weight_ref, total_ref, decay_ref, *refs):
    count = len(routes)
    gated_refs, pieces = refs[:count], refs[count:-3]
    out_ref, gating_grad_ref, window_ref = refs[-3:]
    window_ref[...] = window_of(decay_ref, total_ref.shape[1])
    for rows, mixed in mixed_rows(pieces, total_ref.shape[0]):
        gating_grad_ref[rows] = total_ref[rows].astype(f32) * mixed
    rows = weight_ref.shape[0] // count
    me = lax.axis_index("chan")
    total = None
    for step in range(count):
        place = look_up([list(routes[step]).index(at) for at in range(count)], me)
        block = weight_ref[pl.ds(pl.multiple_of(place * rows, rows), rows), :]
        term = lax.dot_general(
            gated_refs[step][...], block, (((0,), (0,)), ((), ())), preferred_element_type=f32
        )
        total = term if total is None else total + term
    out_ref[...] = total.astype(out_ref.dtype)


def return_kernel(order, window_ref, *refs):
    pieces, (signal_ref, taps_ref) = refs[:-2], refs[-2:]
    chip = lax.div(lax.axis_index("seq"), 2)
    for step, piece in zip(order, pieces):
        blocks, twice, _ = piece.shape
        owned = twice // 2
        place = lax.bitwise_xor(chip, step) if len(pieces) > 1 else 0
        for source in range(blocks):
            first = pl.multiple_of((place * blocks + source) * owned, owned)
            rows = pl.ds(first, owned)
            signal_ref[rows] = piece[source, :owned].astype(f32)
            taps_ref[rows] = piece[source, owned:].astype(f32) * window_ref[rows]


def padded(array, owned, held):
    if owned == held:
        return array
    blocks, rows, lanes = array.shape
    groups = array.reshape(blocks, rows // owned, owned, lanes)
    groups = jnp.pad(groups, ((0, 0), (0, 0), (0, held - owned), (0, 0)))
    return groups.reshape(blocks, -1, lanes)


def trimmed(array, owned, held):
    if owned == held:
        return array
    blocks, rows, lanes = array.shape
    return array.reshape(blocks, rows // held, held, lanes)[:, :, :owned].reshape(blocks, -1, lanes)


def exchange(array):
    return lax.all_to_all(array, "seq", split_axis=0, concat_axis=0, tiled=True)


def per_device(signal, gating, filter_taps, decay_rates, out_weight, out_grad):
    channels, length = signal.shape
    shards = lax.axis_size("seq")
    parts = lax.axis_size("chan")
    owned = channels // shards
    held = -(-owned // ROWS) * ROWS
    height = (shards + 1) * held
    table = jnp.asarray(within_table(length))
    twiddle = jnp.asarray(twiddle_table(shards, length))
    shape = jax.ShapeDtypeStruct

    routes_2 = [[(i + step) % parts for i in range(parts)] for step in range(parts)]
    routes_1 = [range(4), [3, 2, 1, 0], [1, 3, 0, 2], [2, 0, 3, 1]] if parts == 4 else routes_2

    def shift(array, route):
        return lax.ppermute(array, "chan", list(enumerate(route)))

    rates = decay_rates.reshape(1, channels)
    if owned == held:
        pairs = call(
            send_kernel,
            shape((shards, 2 * owned, length), bf16),
            [ANY] * 3,
            (
                pltpu.VMEM((1, channels), f32),
                pltpu.VMEM((channels, length), f32),
                pltpu.VMEM((channels, length), bf16),
                pltpu.SemaphoreType.DMA((3,)),
            ),
            room=62,
        )(rates, filter_taps, signal)
    else:
        pairs = send_plain(decay_rates, filter_taps, signal, shards)
    arrived = exchange(pairs)

    partial = call(
        functools.partial(spread_kernel, routes_1),
        tuple(shape((channels, length), bf16) for k in range(parts)),
        [VMEM] * 2,
        after=(pairs,),
    )(out_weight, out_grad)
    shares = [shift(partial[step], routes_1[step]) for step in range(1, parts)]

    mixed_owned, *spectra = call(
        convolve_kernel,
        (shape((shards, held, length), bf16),) + 4 * (shape((height, length), bf16),),
        [VMEM] * 3,
        (
            pltpu.VMEM((2 * height, 2 * length), bf16),
            pltpu.VMEM((height, 2 * length), f32),
        ),
        micros=2,
    )(padded(arrived, owned, held), table, twiddle)
    chips = shards // 2
    direct = chips in (2, 4) and owned == held

    def hop(array, distance):
        return lax.ppermute(array, "seq", [(i, i ^ distance) for i in range(shards)])

    def bring(array):
        if not direct:
            return [exchange(array)]
        pairs = [[2 * chip, 2 * chip + 1] for chip in range(chips)]
        both = lax.all_gather(array, "seq", axis_index_groups=pairs)
        packed = call(
            pack_kernel, (shape((2,) + array.shape[1:], bf16),) * chips, [VMEM], micros=0
        )(both)
        return [packed[0]] + [hop(packed[step], 2 * step) for step in range(1, chips)]

    pieces = bring(trimmed(mixed_owned, owned, held))

    total, grad_mixed = call(
        total_kernel,
        (shape((channels, length), bf16),) * 2,
        [VMEM] * (2 + len(shares)),
        after=(pieces[0],),
    )(gating, partial[0], *shares)
    grad_whole = exchange(grad_mixed.reshape(shards, owned, length))

    gated = call(gate_kernel, shape((channels, length), bf16), [VMEM] * (1 + len(pieces)))(
        gating, *pieces
    )
    gathered = [gated] + [shift(gated, routes_2[step]) for step in range(1, parts)]
    mixed_out, gating_grad, window = call(
        functools.partial(project_kernel, routes_2),
        (
            shape((length, out_weight.shape[1]), bf16),
            shape((channels, length), f32),
            shape((channels, length), f32),
        ),
        [VMEM] * (3 + parts + len(pieces)),
        micros=12.0,
    )(out_weight, total, rates, *gathered, *pieces)

    grads_owned = call(
        correlate_kernel,
        shape((shards, 2 * held, length), bf16),
        [VMEM] * 7,
        (
            pltpu.VMEM((2 * height, 2 * length), bf16),
            pltpu.VMEM((2 * height, 2 * length), f32),
        ),
        micros=2.0,
        after=(gated,),
    )(padded(grad_whole, owned, held), *spectra, table, twiddle)
    returned = bring(trimmed(grads_owned, owned, held))
    order = (0, 2, 3, 1) if len(returned) == 4 else range(len(returned))
    if owned == held:
        signal_grad, taps_grad = call(
            functools.partial(return_kernel, order),
            (shape((channels, length), f32), shape((channels, length), f32)),
            [VMEM] * (1 + len(returned)),
        )(window, *(returned[step] for step in order))
    else:
        both = returned[0].reshape(shards, 2, owned, length).astype(f32)
        signal_grad = both[:, 0].reshape(channels, length)
        taps_grad = both[:, 1].reshape(channels, length) * window
    return (mixed_out, signal_grad, gating_grad, taps_grad)


def send_plain(decay_rates, filter_taps, signal, shards):
    channels, length = signal.shape
    owned = channels // shards
    places = (lax.axis_index("seq") * length + jnp.arange(length, dtype=jnp.int32)).astype(f32)
    rates = decay_rates[:, None]
    window = jnp.exp(-rates * places[None, :]) * jnp.sqrt(2.0 * rates)
    filters = (filter_taps * window).astype(bf16)
    pairs = jnp.stack([part.reshape(shards, owned, length) for part in (signal, filters)], 1)
    return pairs.reshape(shards, 2 * owned, length)


def solution(mesh):
    in_specs = (
        P("chan", "seq"),
        P("chan", "seq"),
        P("chan", "seq"),
        P("chan"),
        P(None, "chan"),
        P("seq", "chan"),
    )
    out_specs = (P("seq", "chan"), P("chan", "seq"), P("chan", "seq"), P("chan", "seq"))
    return jax.shard_map(
        per_device, mesh=mesh, in_specs=in_specs, out_specs=out_specs, check_vma=False
    )
```

```python
import functools

import jax
import jax.numpy as jnp
import ml_dtypes
import numpy as np
from jax import lax
from jax.experimental import pallas as pl
from jax.experimental.pallas import tpu as pltpu
from jax.sharding import PartitionSpec as P

f32 = jnp.float32
bf16 = jnp.bfloat16
VMEM = pl.BlockSpec(memory_space=pltpu.VMEM)
ANY = pl.BlockSpec(memory_space=pl.ANY)
PEAK_FLOPS_A_MICRO = 1.15e9
ROWS = 16
LANES = 128


def call(kernel, out_shape, in_specs, scratch=(), micros=1, room=16, after=()):
    count = len(in_specs)

    def body(*refs):
        kernel(*refs[:count], *refs[count + len(after) :])

    run = pl.pallas_call(
        body,
        out_shape=out_shape,
        in_specs=list(in_specs) + [ANY] * len(after),
        out_specs=jax.tree.map(lambda _: VMEM, out_shape),
        scratch_shapes=list(scratch),
        cost_estimate=pl.CostEstimate(
            flops=int(micros * PEAK_FLOPS_A_MICRO), bytes_accessed=0, transcendentals=0
        ),
        compiler_params=pltpu.CompilerParams(vmem_limit_bytes=room * 1024 * 1024),
    )
    return lambda *operands: run(*operands, *after)


def within_table(lanes):
    index = np.arange(lanes)
    angle = 2.0 * np.pi * (np.outer(index, index) % lanes) / lanes
    cos, sin = np.cos(angle), np.sin(angle)
    table = np.concatenate(
        [np.concatenate([cos, -sin], 1), np.concatenate([sin, cos], 1)], 0
    )
    return table.astype(ml_dtypes.bfloat16)


def twiddle_table(blocks, lanes):
    rows = np.arange(blocks + 1)[:, None]
    angle = 2.0 * np.pi * rows * np.arange(lanes)[None, :] / (2 * blocks * lanes)
    return np.stack([np.cos(angle), np.sin(angle)], 1).astype(np.float32)


def turned(real, imag, turn, size):
    angle = 2.0 * np.pi * turn / size
    cos, sin = float(np.cos(angle)), float(np.sin(angle))
    if turn == 0:
        return real, imag
    if abs(abs(cos) - abs(sin)) < 1e-9:
        root = abs(cos)
        cs, ss = (1 if cos > 0 else -1), (1 if sin > 0 else -1)
        first = real if cs > 0 else -real
        if cs == ss:
            return (root * cs) * (real - imag), (root * cs) * (real + imag)
        return (root * cs) * (real + imag), (root * cs) * (imag - real)
    return cos * real - sin * imag, sin * real + cos * imag


def real_forward(tiles, size):
    if size == 2:
        return [(tiles[0], None), (tiles[0], None)]
    even = real_forward(tiles[0::2], size // 2)
    odd = real_forward(tiles[1::2], size // 2)
    quarter = size // 4
    out = [None] * (size // 2 + 1)
    out[0] = (even[0][0] + odd[0][0], None)
    out[size // 2] = (even[0][0] - odd[0][0], None)
    for row in range(1, quarter):
        real, imag = turned(odd[row][0], odd[row][1], -row, size)
        out[row] = (even[row][0] + real, even[row][1] + imag)
        out[size // 2 - row] = (even[row][0] - real, imag - even[row][1])
    out[quarter] = (even[quarter][0], -odd[quarter][0])
    return out


def real_inverse(rows, size):
    if size == 2:
        return [rows[0][0] + rows[1][0]]
    quarter = size // 4
    even, odd = [], []
    for row in range(quarter + 1):
        real, imag = rows[row]
        if row == 0:
            last = rows[size // 2][0]
            even.append((real + last, None))
            odd.append((real - last, None))
        elif row == quarter:
            even.append((2.0 * real, None))
            odd.append((-2.0 * imag, None))
        else:
            far_real, far_imag = rows[size // 2 - row]
            even.append((real + far_real, imag - far_imag))
            odd.append(turned(real - far_real, imag + far_imag, row, size))
    firsts = real_inverse(even, size // 2)
    seconds = real_inverse(odd, size // 2)
    return [tile for pair in zip(firsts, seconds) for tile in pair]


def tile_slices(rows, lanes):
    for row in range(0, rows, ROWS):
        for lane in range(0, lanes, LANES):
            yield row, lane


def first_step(read, twiddle_ref, out_ref, base, blocks, rows, lanes):
    for row, lane in tile_slices(rows, lanes):
        tiles = [read(block, row, lane) for block in range(blocks)]
        for step, (real, imag) in enumerate(real_forward(tiles, 2 * blocks)):
            cos = twiddle_ref[step, 0:1, lane : lane + LANES]
            sin = twiddle_ref[step, 1:2, lane : lane + LANES]
            if step == 0:
                new_real, new_imag = real, jnp.zeros_like(real)
            elif imag is None:
                new_real, new_imag = real * cos, -real * sin
            else:
                new_real, new_imag = real * cos + imag * sin, imag * cos - real * sin
            at = base + step * rows + row
            out_ref[at : at + ROWS, lane : lane + LANES] = new_real.astype(bf16)
            out_ref[at : at + ROWS, lanes + lane : lanes + lane + LANES] = new_imag.astype(bf16)


def last_step(spec_ref, base, twiddle_ref, write, blocks, rows, lanes):
    scale = 1.0 / (2 * blocks * lanes)
    for row, lane in tile_slices(rows, lanes):
        steps = []
        for step in range(blocks + 1):
            at = base + step * rows + row
            imag = spec_ref[at : at + ROWS, lane : lane + LANES]
            real = spec_ref[at : at + ROWS, lanes + lane : lanes + lane + LANES]
            cos = twiddle_ref[step, 0:1, lane : lane + LANES] * scale
            sin = twiddle_ref[step, 1:2, lane : lane + LANES] * scale
            new_real = real * cos - imag * sin
            if step == 0 or step == blocks:
                steps.append((new_real, None))
            else:
                steps.append((new_real, imag * cos + real * sin))
        for block, tile in enumerate(real_inverse(steps, 2 * blocks)):
            write(block, row, lane, tile)


def tile_read(ref, base):
    def read(block, row, lane):
        at = base + row
        return ref[block, at : at + ROWS, lane : lane + LANES].astype(f32)

    return read


def tile_write(ref, base):
    def write(block, row, lane, tile):
        at = base + row
        ref[block, at : at + ROWS, lane : lane + LANES] = tile.astype(ref.dtype)

    return write


def product(first_real, first_imag, second_real, second_imag, out_ref, base, conjugate):
    rows, lanes = first_real.shape
    if conjugate:
        real = first_real * second_real + first_imag * second_imag
        imag = first_imag * second_real - first_real * second_imag
    else:
        real = first_real * second_real - first_imag * second_imag
        imag = first_real * second_imag + first_imag * second_real
    out_ref[base : base + rows, :lanes] = imag.astype(bf16)
    out_ref[base : base + rows, lanes:] = real.astype(bf16)


def convolve_kernel(
    pair_ref,
    table_ref,
    twiddle_ref,
    mixed_ref,
    signal_real,
    signal_imag,
    filter_real,
    filter_imag,
    left_ref,
    back_ref,
):
    blocks, rows, lanes = mixed_ref.shape
    height = (blocks + 1) * rows
    first_step(tile_read(pair_ref, 0), twiddle_ref, left_ref, 0, blocks, rows, lanes)
    first_step(tile_read(pair_ref, rows), twiddle_ref, left_ref, height, blocks, rows, lanes)
    spectra = []
    for base, real_ref, imag_ref in (
        (0, signal_real, signal_imag),
        (height, filter_real, filter_imag),
    ):
        spectrum = jnp.dot(
            left_ref[base : base + height], table_ref[...], preferred_element_type=f32
        )
        real_ref[...] = spectrum[:, :lanes].astype(bf16)
        imag_ref[...] = spectrum[:, lanes:].astype(bf16)
        spectra.append(spectrum)
    product(
        spectra[0][:, :lanes],
        spectra[0][:, lanes:],
        spectra[1][:, :lanes],
        spectra[1][:, lanes:],
        left_ref,
        0,
        False,
    )
    back_ref[...] = jnp.dot(left_ref[:height], table_ref[...], preferred_element_type=f32)
    last_step(back_ref, 0, twiddle_ref, tile_write(mixed_ref, 0), blocks, rows, lanes)


def correlate_kernel(
    grad_ref,
    signal_real,
    signal_imag,
    filter_real,
    filter_imag,
    table_ref,
    twiddle_ref,
    out_ref,
    left_ref,
    back_ref,
):
    blocks, rows, lanes = grad_ref.shape
    height = (blocks + 1) * rows
    first_step(tile_read(grad_ref, 0), twiddle_ref, left_ref, 0, blocks, rows, lanes)
    grad = jnp.dot(left_ref[:height], table_ref[...], preferred_element_type=f32)
    for base, real_ref, imag_ref in (
        (0, filter_real, filter_imag),
        (height, signal_real, signal_imag),
    ):
        product(
            grad[:, :lanes],
            grad[:, lanes:],
            real_ref[...].astype(f32),
            imag_ref[...].astype(f32),
            left_ref,
            base,
            True,
        )
    back_ref[...] = jnp.dot(left_ref[...], table_ref[...], preferred_element_type=f32)
    last_step(back_ref, 0, twiddle_ref, tile_write(out_ref, 0), blocks, rows, lanes)
    last_step(back_ref, height, twiddle_ref, tile_write(out_ref, rows), blocks, rows, lanes)


def window_of(decay_ref, length):
    channels = decay_ref.shape[1]
    start = lax.axis_index("seq") * length
    places = (start + lax.broadcasted_iota(jnp.int32, (1, length), 1)).astype(f32)
    rates = jnp.broadcast_to(decay_ref[...], (length, channels)).T
    return jnp.exp(-rates * places) * jnp.sqrt(2.0 * rates)


def send_kernel(decay_in, taps_in, signal_in, pair_ref, decay_ref, taps_ref, signal_ref, sems):
    fetches = [
        pltpu.make_async_copy(source, target, sems.at[at])
        for at, (source, target) in enumerate(
            ((decay_in, decay_ref), (taps_in, taps_ref), (signal_in, signal_ref))
        )
    ]
    for fetch in fetches:
        fetch.start()
    shards, twice, length = pair_ref.shape
    owned = twice // 2
    fetches[0].wait()
    window = window_of(decay_ref, length)
    fetches[1].wait()
    fetches[2].wait()
    filters = (taps_ref[...] * window).astype(bf16)
    for shard in range(shards):
        rows = slice(shard * owned, (shard + 1) * owned)
        pair_ref[shard, :owned] = signal_ref[rows]
        pair_ref[shard, owned:] = filters[rows]


def look_up(table, index):
    value = jnp.int32(table[0])
    for at in range(1, len(table)):
        value = jnp.where(index == at, jnp.int32(table[at]), value)
    return value


def spread_kernel(routes, steps, weight_ref, grad_ref, *out_refs):
    count = len(routes)
    rows = weight_ref.shape[0] // count
    me = lax.axis_index("chan")
    for step, out_ref in zip(steps, out_refs):
        place = look_up(routes[step], me)
        block = weight_ref[pl.ds(pl.multiple_of(place * rows, rows), rows), :]
        out_ref[...] = lax.dot_general(
            block, grad_ref[...], (((1,), (1,)), ((), ())), preferred_element_type=f32
        ).astype(out_ref.dtype)


def total_kernel(gating_ref, *refs):
    total_ref, grad_mixed_ref = refs[-2:]
    total = refs[0][...].astype(f32)
    for share in refs[1:-2]:
        total = total + share[...].astype(f32)
    total_ref[...] = total.astype(bf16)
    grad_mixed_ref[...] = (total * gating_ref[...].astype(f32)).astype(bf16)


def pack_kernel(both_ref, *out_refs):
    me = lax.axis_index("seq")
    core = lax.rem(me, 2)
    chip = lax.div(me, 2)
    for step, out_ref in enumerate(out_refs):
        block = 2 * lax.bitwise_xor(chip, step) + core
        for source in range(2):
            out_ref[source] = both_ref[source, block]


def mixed_rows(pieces, channels):
    chip = lax.div(lax.axis_index("seq"), 2)
    count = channels // len(pieces)
    for step, piece in enumerate(pieces):
        place = lax.bitwise_xor(chip, step) if len(pieces) > 1 else 0
        rows = pl.ds(pl.multiple_of(place * count, count), count)
        yield rows, piece[...].reshape(count, -1).astype(f32)


def gate_kernel(gating_ref, *refs):
    for rows, mixed in mixed_rows(refs[:-1], gating_ref.shape[0]):
        refs[-1][rows] = (gating_ref[rows].astype(f32) * mixed).astype(bf16)


def project_kernel(routes, weight_ref, total_ref, decay_ref, *refs):
    count = len(routes)
    gated_refs, pieces = refs[:count], refs[count:-3]
    out_ref, gating_grad_ref, window_ref = refs[-3:]
    window_ref[...] = window_of(decay_ref, total_ref.shape[1])
    for rows, mixed in mixed_rows(pieces, total_ref.shape[0]):
        gating_grad_ref[rows] = total_ref[rows].astype(f32) * mixed
    rows = weight_ref.shape[0] // count
    me = lax.axis_index("chan")
    total = None
    for step in range(count):
        place = look_up([list(routes[step]).index(at) for at in range(count)], me)
        block = weight_ref[pl.ds(pl.multiple_of(place * rows, rows), rows), :]
        term = lax.dot_general(
            gated_refs[step][...], block, (((0,), (0,)), ((), ())), preferred_element_type=f32
        )
        total = term if total is None else total + term
    out_ref[...] = total.astype(out_ref.dtype)


def return_kernel(order, window_ref, *refs):
    pieces, (signal_ref, taps_ref) = refs[:-2], refs[-2:]
    chip = lax.div(lax.axis_index("seq"), 2)
    for step, piece in zip(order, pieces):
        blocks, twice, _ = piece.shape
        owned = twice // 2
        place = lax.bitwise_xor(chip, step) if len(pieces) > 1 else 0
        for source in range(blocks):
            first = pl.multiple_of((place * blocks + source) * owned, owned)
            rows = pl.ds(first, owned)
            signal_ref[rows] = piece[source, :owned].astype(f32)
            taps_ref[rows] = piece[source, owned:].astype(f32) * window_ref[rows]


def padded(array, owned, held):
    if owned == held:
        return array
    blocks, rows, lanes = array.shape
    groups = array.reshape(blocks, rows // owned, owned, lanes)
    groups = jnp.pad(groups, ((0, 0), (0, 0), (0, held - owned), (0, 0)))
    return groups.reshape(blocks, -1, lanes)


def trimmed(array, owned, held):
    if owned == held:
        return array
    blocks, rows, lanes = array.shape
    return array.reshape(blocks, rows // held, held, lanes)[:, :, :owned].reshape(blocks, -1, lanes)


def exchange(array):
    return lax.all_to_all(array, "seq", split_axis=0, concat_axis=0, tiled=True)


def per_device(signal, gating, filter_taps, decay_rates, out_weight, out_grad):
    channels, length = signal.shape
    shards = lax.axis_size("seq")
    parts = lax.axis_size("chan")
    owned = channels // shards
    held = -(-owned // ROWS) * ROWS
    height = (shards + 1) * held
    table = jnp.asarray(within_table(length))
    twiddle = jnp.asarray(twiddle_table(shards, length))
    shape = jax.ShapeDtypeStruct

    routes_2 = [[(i - step) % parts for i in range(parts)] for step in range(parts)]
    routes_1 = [range(4), [3, 2, 1, 0], [1, 3, 0, 2], [2, 0, 3, 1]] if parts == 4 else routes_2

    def shift(array, route):
        return lax.ppermute(array, "chan", list(enumerate(route)))

    rates = decay_rates.reshape(1, channels)
    if owned == held:
        pairs = call(
            send_kernel,
            shape((shards, 2 * owned, length), bf16),
            [ANY] * 3,
            (
                pltpu.VMEM((1, channels), f32),
                pltpu.VMEM((channels, length), f32),
                pltpu.VMEM((channels, length), bf16),
                pltpu.SemaphoreType.DMA((3,)),
            ),
            room=62,
        )(rates, filter_taps, signal)
    else:
        pairs = send_plain(decay_rates, filter_taps, signal, shards)
    arrived = exchange(pairs)

    part = shape((channels, length), bf16)
    (first,) = call(functools.partial(spread_kernel, routes_1, [1]), (part,), [VMEM] * 2)(
        out_weight, out_grad
    )
    rest = list(range(2, parts)) + [0]
    others = call(
        functools.partial(spread_kernel, routes_1, rest),
        (part,) * len(rest),
        [VMEM] * 2,
        after=(first,),
    )(out_weight, out_grad)
    partial = [others[-1], first, *others[:-1]]
    shares = [shift(partial[step], routes_1[step]) for step in range(1, parts)]

    mixed_owned, *spectra = call(
        convolve_kernel,
        (shape((shards, held, length), bf16),) + 4 * (shape((height, length), bf16),),
        [VMEM] * 3,
        (
            pltpu.VMEM((2 * height, 2 * length), bf16),
            pltpu.VMEM((height, 2 * length), f32),
        ),
        micros=2,
    )(padded(arrived, owned, held), table, twiddle)
    chips = shards // 2
    direct = chips in (2, 4) and owned == held

    def hop(array, distance):
        return lax.ppermute(array, "seq", [(i, i ^ distance) for i in range(shards)])

    def bring(array):
        if not direct:
            return [exchange(array)]
        pairs = [[2 * chip, 2 * chip + 1] for chip in range(chips)]
        both = lax.all_gather(array, "seq", axis_index_groups=pairs)
        packed = call(
            pack_kernel, (shape((2,) + array.shape[1:], bf16),) * chips, [VMEM], micros=0
        )(both)
        return [packed[0]] + [hop(packed[step], 2 * step) for step in range(1, chips)]

    pieces = bring(trimmed(mixed_owned, owned, held))

    total, grad_mixed = call(
        total_kernel,
        (shape((channels, length), bf16),) * 2,
        [VMEM] * (2 + len(shares)),
        after=(pieces[0],),
    )(gating, partial[0], *shares)
    grad_whole = exchange(grad_mixed.reshape(shards, owned, length))

    gated = call(gate_kernel, shape((channels, length), bf16), [VMEM] * (1 + len(pieces)))(
        gating, *pieces
    )
    gathered = [gated] + [shift(gated, routes_2[step]) for step in range(1, parts)]
    mixed_out, gating_grad, window = call(
        functools.partial(project_kernel, routes_2),
        (
            shape((length, out_weight.shape[1]), bf16),
            shape((channels, length), f32),
            shape((channels, length), f32),
        ),
        [VMEM] * (3 + parts + len(pieces)),
        micros=12.0,
    )(out_weight, total, rates, *gathered, *pieces)

    grads_owned = call(
        correlate_kernel,
        shape((shards, 2 * held, length), bf16),
        [VMEM] * 7,
        (
            pltpu.VMEM((2 * height, 2 * length), bf16),
            pltpu.VMEM((2 * height, 2 * length), f32),
        ),
        micros=2.0,
        after=(gated,),
    )(padded(grad_whole, owned, held), *spectra, table, twiddle)
    returned = bring(trimmed(grads_owned, owned, held))
    order = (0, 2, 3, 1) if len(returned) == 4 else range(len(returned))
    if owned == held:
        signal_grad, taps_grad = call(
            functools.partial(return_kernel, order),
            (shape((channels, length), f32), shape((channels, length), f32)),
            [VMEM] * (1 + len(returned)),
        )(window, *(returned[step] for step in order))
    else:
        both = returned[0].reshape(shards, 2, owned, length).astype(f32)
        signal_grad = both[:, 0].reshape(channels, length)
        taps_grad = both[:, 1].reshape(channels, length) * window
    return (mixed_out, signal_grad, gating_grad, taps_grad)


def send_plain(decay_rates, filter_taps, signal, shards):
    channels, length = signal.shape
    owned = channels // shards
    places = (lax.axis_index("seq") * length + jnp.arange(length, dtype=jnp.int32)).astype(f32)
    rates = decay_rates[:, None]
    window = jnp.exp(-rates * places[None, :]) * jnp.sqrt(2.0 * rates)
    filters = (filter_taps * window).astype(bf16)
    pairs = jnp.stack([part.reshape(shards, owned, length) for part in (signal, filters)], 1)
    return pairs.reshape(shards, 2 * owned, length)


def solution(mesh):
    in_specs = (
        P("chan", "seq"),
        P("chan", "seq"),
        P("chan", "seq"),
        P("chan"),
        P(None, "chan"),
        P("seq", "chan"),
    )
    out_specs = (P("seq", "chan"), P("chan", "seq"), P("chan", "seq"), P("chan", "seq"))
    return jax.shard_map(
        per_device, mesh=mesh, in_specs=in_specs, out_specs=out_specs, check_vma=False
    )
```

```python
import functools

import jax
import jax.numpy as jnp
import ml_dtypes
import numpy as np
from jax import lax
from jax.experimental import pallas as pl
from jax.experimental.pallas import tpu as pltpu
from jax.sharding import PartitionSpec as P

f32 = jnp.float32
bf16 = jnp.bfloat16
VMEM = pl.BlockSpec(memory_space=pltpu.VMEM)
ANY = pl.BlockSpec(memory_space=pl.ANY)
PEAK_FLOPS_A_MICRO = 1.15e9
ROWS = 16
LANES = 128


def call(kernel, out_shape, in_specs, scratch=(), micros=1, room=16, after=()):
    count = len(in_specs)

    def body(*refs):
        kernel(*refs[:count], *refs[count + len(after) :])

    run = pl.pallas_call(
        body,
        out_shape=out_shape,
        in_specs=list(in_specs) + [ANY] * len(after),
        out_specs=jax.tree.map(lambda _: VMEM, out_shape),
        scratch_shapes=list(scratch),
        cost_estimate=pl.CostEstimate(
            flops=int(micros * PEAK_FLOPS_A_MICRO), bytes_accessed=0, transcendentals=0
        ),
        compiler_params=pltpu.CompilerParams(vmem_limit_bytes=room * 1024 * 1024),
    )
    return lambda *operands: run(*operands, *after)


def within_table(lanes):
    index = np.arange(lanes)
    angle = 2.0 * np.pi * (np.outer(index, index) % lanes) / lanes
    cos, sin = np.cos(angle), np.sin(angle)
    table = np.concatenate(
        [np.concatenate([cos, -sin], 1), np.concatenate([sin, cos], 1)], 0
    )
    return table.astype(ml_dtypes.bfloat16)


def twiddle_table(blocks, lanes):
    rows = np.arange(blocks + 1)[:, None]
    angle = 2.0 * np.pi * rows * np.arange(lanes)[None, :] / (2 * blocks * lanes)
    return np.stack([np.cos(angle), np.sin(angle)], 1).astype(np.float32)


def turned(real, imag, turn, size):
    angle = 2.0 * np.pi * turn / size
    cos, sin = float(np.cos(angle)), float(np.sin(angle))
    if turn == 0:
        return real, imag
    if abs(abs(cos) - abs(sin)) < 1e-9:
        root = abs(cos)
        cs, ss = (1 if cos > 0 else -1), (1 if sin > 0 else -1)
        first = real if cs > 0 else -real
        if cs == ss:
            return (root * cs) * (real - imag), (root * cs) * (real + imag)
        return (root * cs) * (real + imag), (root * cs) * (imag - real)
    return cos * real - sin * imag, sin * real + cos * imag


def real_forward(tiles, size):
    if size == 2:
        return [(tiles[0], None), (tiles[0], None)]
    even = real_forward(tiles[0::2], size // 2)
    odd = real_forward(tiles[1::2], size // 2)
    quarter = size // 4
    out = [None] * (size // 2 + 1)
    out[0] = (even[0][0] + odd[0][0], None)
    out[size // 2] = (even[0][0] - odd[0][0], None)
    for row in range(1, quarter):
        real, imag = turned(odd[row][0], odd[row][1], -row, size)
        out[row] = (even[row][0] + real, even[row][1] + imag)
        out[size // 2 - row] = (even[row][0] - real, imag - even[row][1])
    out[quarter] = (even[quarter][0], -odd[quarter][0])
    return out


def real_inverse(rows, size):
    if size == 2:
        return [rows[0][0] + rows[1][0]]
    quarter = size // 4
    even, odd = [], []
    for row in range(quarter + 1):
        real, imag = rows[row]
        if row == 0:
            last = rows[size // 2][0]
            even.append((real + last, None))
            odd.append((real - last, None))
        elif row == quarter:
            even.append((2.0 * real, None))
            odd.append((-2.0 * imag, None))
        else:
            far_real, far_imag = rows[size // 2 - row]
            even.append((real + far_real, imag - far_imag))
            odd.append(turned(real - far_real, imag + far_imag, row, size))
    firsts = real_inverse(even, size // 2)
    seconds = real_inverse(odd, size // 2)
    return [tile for pair in zip(firsts, seconds) for tile in pair]


def tile_slices(rows, lanes):
    for row in range(0, rows, ROWS):
        for lane in range(0, lanes, LANES):
            yield row, lane


def first_step(read, twiddle_ref, out_ref, base, blocks, rows, lanes):
    for row, lane in tile_slices(rows, lanes):
        tiles = [read(block, row, lane) for block in range(blocks)]
        for step, (real, imag) in enumerate(real_forward(tiles, 2 * blocks)):
            cos = twiddle_ref[step, 0:1, lane : lane + LANES]
            sin = twiddle_ref[step, 1:2, lane : lane + LANES]
            if step == 0:
                new_real, new_imag = real, jnp.zeros_like(real)
            elif imag is None:
                new_real, new_imag = real * cos, -real * sin
            else:
                new_real, new_imag = real * cos + imag * sin, imag * cos - real * sin
            at = base + step * rows + row
            out_ref[at : at + ROWS, lane : lane + LANES] = new_real.astype(bf16)
            out_ref[at : at + ROWS, lanes + lane : lanes + lane + LANES] = new_imag.astype(bf16)


def last_step(spec_ref, base, twiddle_ref, write, blocks, rows, lanes):
    scale = 1.0 / (2 * blocks * lanes)
    for row, lane in tile_slices(rows, lanes):
        steps = []
        for step in range(blocks + 1):
            at = base + step * rows + row
            imag = spec_ref[at : at + ROWS, lane : lane + LANES]
            real = spec_ref[at : at + ROWS, lanes + lane : lanes + lane + LANES]
            cos = twiddle_ref[step, 0:1, lane : lane + LANES] * scale
            sin = twiddle_ref[step, 1:2, lane : lane + LANES] * scale
            new_real = real * cos - imag * sin
            if step == 0 or step == blocks:
                steps.append((new_real, None))
            else:
                steps.append((new_real, imag * cos + real * sin))
        for block, tile in enumerate(real_inverse(steps, 2 * blocks)):
            write(block, row, lane, tile)


def tile_read(ref, base):
    def read(block, row, lane):
        at = base + row
        return ref[block, at : at + ROWS, lane : lane + LANES].astype(f32)

    return read


def tile_write(ref, base):
    def write(block, row, lane, tile):
        at = base + row
        ref[block, at : at + ROWS, lane : lane + LANES] = tile.astype(ref.dtype)

    return write


def product(first_real, first_imag, second_real, second_imag, out_ref, base, conjugate):
    rows, lanes = first_real.shape
    if conjugate:
        real = first_real * second_real + first_imag * second_imag
        imag = first_imag * second_real - first_real * second_imag
    else:
        real = first_real * second_real - first_imag * second_imag
        imag = first_real * second_imag + first_imag * second_real
    out_ref[base : base + rows, :lanes] = imag.astype(bf16)
    out_ref[base : base + rows, lanes:] = real.astype(bf16)


def convolve_kernel(
    pair_ref,
    table_ref,
    twiddle_ref,
    mixed_ref,
    signal_real,
    signal_imag,
    filter_real,
    filter_imag,
    left_ref,
    back_ref,
):
    blocks, rows, lanes = mixed_ref.shape
    height = (blocks + 1) * rows
    first_step(tile_read(pair_ref, 0), twiddle_ref, left_ref, 0, blocks, rows, lanes)
    first_step(tile_read(pair_ref, rows), twiddle_ref, left_ref, height, blocks, rows, lanes)
    spectra = []
    for base, real_ref, imag_ref in (
        (0, signal_real, signal_imag),
        (height, filter_real, filter_imag),
    ):
        spectrum = jnp.dot(
            left_ref[base : base + height], table_ref[...], preferred_element_type=f32
        )
        real_ref[...] = spectrum[:, :lanes].astype(bf16)
        imag_ref[...] = spectrum[:, lanes:].astype(bf16)
        spectra.append(spectrum)
    product(
        spectra[0][:, :lanes],
        spectra[0][:, lanes:],
        spectra[1][:, :lanes],
        spectra[1][:, lanes:],
        left_ref,
        0,
        False,
    )
    back_ref[...] = jnp.dot(left_ref[:height], table_ref[...], preferred_element_type=f32)
    last_step(back_ref, 0, twiddle_ref, tile_write(mixed_ref, 0), blocks, rows, lanes)


def correlate_kernel(
    grad_ref,
    signal_real,
    signal_imag,
    filter_real,
    filter_imag,
    table_ref,
    twiddle_ref,
    out_ref,
    left_ref,
    back_ref,
):
    blocks, rows, lanes = grad_ref.shape
    height = (blocks + 1) * rows
    first_step(tile_read(grad_ref, 0), twiddle_ref, left_ref, 0, blocks, rows, lanes)
    grad = jnp.dot(left_ref[:height], table_ref[...], preferred_element_type=f32)
    for base, real_ref, imag_ref in (
        (0, filter_real, filter_imag),
        (height, signal_real, signal_imag),
    ):
        product(
            grad[:, :lanes],
            grad[:, lanes:],
            real_ref[...].astype(f32),
            imag_ref[...].astype(f32),
            left_ref,
            base,
            True,
        )
    back_ref[...] = jnp.dot(left_ref[...], table_ref[...], preferred_element_type=f32)
    last_step(back_ref, 0, twiddle_ref, tile_write(out_ref, 0), blocks, rows, lanes)
    last_step(back_ref, height, twiddle_ref, tile_write(out_ref, rows), blocks, rows, lanes)


def window_of(decay_ref, length):
    channels = decay_ref.shape[1]
    start = lax.axis_index("seq") * length
    places = (start + lax.broadcasted_iota(jnp.int32, (1, length), 1)).astype(f32)
    rates = jnp.broadcast_to(decay_ref[...], (length, channels)).T
    return jnp.exp(-rates * places) * jnp.sqrt(2.0 * rates)


def send_kernel(decay_in, taps_in, signal_in, pair_ref, decay_ref, taps_ref, signal_ref, sems):
    fetches = [
        pltpu.make_async_copy(source, target, sems.at[at])
        for at, (source, target) in enumerate(
            ((decay_in, decay_ref), (taps_in, taps_ref), (signal_in, signal_ref))
        )
    ]
    for fetch in fetches:
        fetch.start()
    shards, twice, length = pair_ref.shape
    owned = twice // 2
    fetches[0].wait()
    window = window_of(decay_ref, length)
    fetches[1].wait()
    fetches[2].wait()
    filters = (taps_ref[...] * window).astype(bf16)
    for shard in range(shards):
        rows = slice(shard * owned, (shard + 1) * owned)
        pair_ref[shard, :owned] = signal_ref[rows]
        pair_ref[shard, owned:] = filters[rows]


def look_up(table, index):
    value = jnp.int32(table[0])
    for at in range(1, len(table)):
        value = jnp.where(index == at, jnp.int32(table[at]), value)
    return value


def spread_kernel(routes, weight_ref, grad_ref, *out_refs):
    count = len(out_refs)
    rows = weight_ref.shape[0] // count
    me = lax.axis_index("chan")
    for step in list(range(1, count)) + [0]:
        place = look_up(routes[step], me)
        block = weight_ref[pl.ds(pl.multiple_of(place * rows, rows), rows), :]
        out_refs[step][...] = lax.dot_general(
            block, grad_ref[...], (((1,), (1,)), ((), ())), preferred_element_type=f32
        ).astype(out_refs[step].dtype)


def total_kernel(gating_ref, *refs):
    total_ref, grad_mixed_ref = refs[-2:]
    total = refs[0][...].astype(f32)
    for share in refs[1:-2]:
        total = total + share[...].astype(f32)
    total_ref[...] = total.astype(bf16)
    grad_mixed_ref[...] = (total * gating_ref[...].astype(f32)).astype(bf16)


def pack_kernel(both_ref, *out_refs):
    me = lax.axis_index("seq")
    core = lax.rem(me, 2)
    chip = lax.div(me, 2)
    for step, out_ref in enumerate(out_refs):
        block = 2 * lax.bitwise_xor(chip, step) + core
        for source in range(2):
            out_ref[source] = both_ref[source, block]


def mixed_rows(pieces, channels):
    chip = lax.div(lax.axis_index("seq"), 2)
    count = channels // len(pieces)
    for step, piece in enumerate(pieces):
        place = lax.bitwise_xor(chip, step) if len(pieces) > 1 else 0
        rows = pl.ds(pl.multiple_of(place * count, count), count)
        yield rows, piece[...].reshape(count, -1).astype(f32)


def gate_kernel(gating_ref, *refs):
    for rows, mixed in mixed_rows(refs[:-1], gating_ref.shape[0]):
        refs[-1][rows] = (gating_ref[rows].astype(f32) * mixed).astype(bf16)


def project_kernel(routes, weight_ref, total_ref, decay_ref, *refs):
    count = len(routes)
    gated_refs, pieces = refs[:count], refs[count:-3]
    out_ref, gating_grad_ref, window_ref = refs[-3:]
    window_ref[...] = window_of(decay_ref, total_ref.shape[1])
    for rows, mixed in mixed_rows(pieces, total_ref.shape[0]):
        gating_grad_ref[rows] = total_ref[rows].astype(f32) * mixed
    rows = weight_ref.shape[0] // count
    me = lax.axis_index("chan")
    total = None
    for step in range(count):
        place = look_up([list(routes[step]).index(at) for at in range(count)], me)
        block = weight_ref[pl.ds(pl.multiple_of(place * rows, rows), rows), :]
        term = lax.dot_general(
            gated_refs[step][...], block, (((0,), (0,)), ((), ())), preferred_element_type=f32
        )
        total = term if total is None else total + term
    out_ref[...] = total.astype(out_ref.dtype)


def return_kernel(order, window_ref, *refs):
    pieces, (signal_ref, taps_ref) = refs[:-2], refs[-2:]
    chip = lax.div(lax.axis_index("seq"), 2)
    for step, piece in zip(order, pieces):
        blocks, twice, _ = piece.shape
        owned = twice // 2
        place = lax.bitwise_xor(chip, step) if len(pieces) > 1 else 0
        for source in range(blocks):
            first = pl.multiple_of((place * blocks + source) * owned, owned)
            rows = pl.ds(first, owned)
            signal_ref[rows] = piece[source, :owned].astype(f32)
            taps_ref[rows] = piece[source, owned:].astype(f32) * window_ref[rows]


def padded(array, owned, held):
    if owned == held:
        return array
    blocks, rows, lanes = array.shape
    groups = array.reshape(blocks, rows // owned, owned, lanes)
    groups = jnp.pad(groups, ((0, 0), (0, 0), (0, held - owned), (0, 0)))
    return groups.reshape(blocks, -1, lanes)


def trimmed(array, owned, held):
    if owned == held:
        return array
    blocks, rows, lanes = array.shape
    return array.reshape(blocks, rows // held, held, lanes)[:, :, :owned].reshape(blocks, -1, lanes)


def exchange(array):
    return lax.all_to_all(array, "seq", split_axis=0, concat_axis=0, tiled=True)


def per_device(signal, gating, filter_taps, decay_rates, out_weight, out_grad):
    channels, length = signal.shape
    shards = lax.axis_size("seq")
    parts = lax.axis_size("chan")
    owned = channels // shards
    held = -(-owned // ROWS) * ROWS
    height = (shards + 1) * held
    table = jnp.asarray(within_table(length))
    twiddle = jnp.asarray(twiddle_table(shards, length))
    shape = jax.ShapeDtypeStruct

    routes_2 = [[(i + step) % parts for i in range(parts)] for step in range(parts)]
    routes_1 = [range(4), [3, 2, 1, 0], [1, 3, 0, 2], [2, 0, 3, 1]] if parts == 4 else routes_2

    def shift(array, route):
        return lax.ppermute(array, "chan", list(enumerate(route)))

    rates = decay_rates.reshape(1, channels)
    if owned == held:
        pairs = call(
            send_kernel,
            shape((shards, 2 * owned, length), bf16),
            [ANY] * 3,
            (
                pltpu.VMEM((1, channels), f32),
                pltpu.VMEM((channels, length), f32),
                pltpu.VMEM((channels, length), bf16),
                pltpu.SemaphoreType.DMA((3,)),
            ),
            room=62,
        )(rates, filter_taps, signal)
    else:
        pairs = send_plain(decay_rates, filter_taps, signal, shards)
    arrived = exchange(pairs)

    partial = call(
        functools.partial(spread_kernel, routes_1),
        tuple(shape((channels, length), bf16) for k in range(parts)),
        [VMEM] * 2,
    )(out_weight, out_grad)
    shares = [shift(partial[step], routes_1[step]) for step in range(1, parts)]

    mixed_owned, *spectra = call(
        convolve_kernel,
        (shape((shards, held, length), bf16),) + 4 * (shape((height, length), bf16),),
        [VMEM] * 3,
        (
            pltpu.VMEM((2 * height, 2 * length), bf16),
            pltpu.VMEM((height, 2 * length), f32),
        ),
        micros=2,
    )(padded(arrived, owned, held), table, twiddle)
    chips = shards // 2
    direct = chips in (2, 4) and owned == held

    def hop(array, distance):
        return lax.ppermute(array, "seq", [(i, i ^ distance) for i in range(shards)])

    def bring(array):
        if not direct:
            return [exchange(array)]
        pairs = [[2 * chip, 2 * chip + 1] for chip in range(chips)]
        both = lax.all_gather(array, "seq", axis_index_groups=pairs)
        packed = call(
            pack_kernel, (shape((2,) + array.shape[1:], bf16),) * chips, [VMEM], micros=0
        )(both)
        return [packed[0]] + [hop(packed[step], 2 * step) for step in range(1, chips)]

    pieces = bring(trimmed(mixed_owned, owned, held))

    total, grad_mixed = call(
        total_kernel,
        (shape((channels, length), bf16),) * 2,
        [VMEM] * (2 + len(shares)),
        after=(pieces[0],),
    )(gating, partial[0], *shares)
    grad_whole = exchange(grad_mixed.reshape(shards, owned, length))

    gated = call(gate_kernel, shape((channels, length), bf16), [VMEM] * (1 + len(pieces)))(
        gating, *pieces
    )
    gathered = [gated] + [shift(gated, routes_2[step]) for step in range(1, parts)]
    mixed_out, gating_grad, window = call(
        functools.partial(project_kernel, routes_2),
        (
            shape((length, out_weight.shape[1]), bf16),
            shape((channels, length), f32),
            shape((channels, length), f32),
        ),
        [VMEM] * (3 + parts + len(pieces)),
        micros=12.0,
    )(out_weight, total, rates, *gathered, *pieces)

    grads_owned = call(
        correlate_kernel,
        shape((shards, 2 * held, length), bf16),
        [VMEM] * 7,
        (
            pltpu.VMEM((2 * height, 2 * length), bf16),
            pltpu.VMEM((2 * height, 2 * length), f32),
        ),
        micros=2.0,
        after=(gated,),
    )(padded(grad_whole, owned, held), *spectra, table, twiddle)
    returned = bring(trimmed(grads_owned, owned, held))
    order = (0, 2, 3, 1) if len(returned) == 4 else range(len(returned))
    if owned == held:
        signal_grad, taps_grad = call(
            functools.partial(return_kernel, order),
            (shape((channels, length), f32), shape((channels, length), f32)),
            [VMEM] * (1 + len(returned)),
        )(window, *(returned[step] for step in order))
    else:
        both = returned[0].reshape(shards, 2, owned, length).astype(f32)
        signal_grad = both[:, 0].reshape(channels, length)
        taps_grad = both[:, 1].reshape(channels, length) * window
    return (mixed_out, signal_grad, gating_grad, taps_grad)


def send_plain(decay_rates, filter_taps, signal, shards):
    channels, length = signal.shape
    owned = channels // shards
    places = (lax.axis_index("seq") * length + jnp.arange(length, dtype=jnp.int32)).astype(f32)
    rates = decay_rates[:, None]
    window = jnp.exp(-rates * places[None, :]) * jnp.sqrt(2.0 * rates)
    filters = (filter_taps * window).astype(bf16)
    pairs = jnp.stack([part.reshape(shards, owned, length) for part in (signal, filters)], 1)
    return pairs.reshape(shards, 2 * owned, length)


def solution(mesh):
    in_specs = (
        P("chan", "seq"),
        P("chan", "seq"),
        P("chan", "seq"),
        P("chan"),
        P(None, "chan"),
        P("seq", "chan"),
    )
    out_specs = (P("seq", "chan"), P("chan", "seq"), P("chan", "seq"), P("chan", "seq"))
    return jax.shard_map(
        per_device, mesh=mesh, in_specs=in_specs, out_specs=out_specs, check_vma=False
    )
```
